32 devices in a mesh: cases: 2 (over y), blocks: 4 (over z), split: 2 (over x), inner: 2 (over core).
Axes of the slice: x: 2, y: 2, z: 4, core: 2. Of those that a mesh axis runs over, the one named last changes fastest.
Arguments:
- state: float32 [5, 64, 16, 256], P(None, ('cases', 'blocks', 'split', 'inner')), parts along dimension 1, may hold values from -2 to 5, as said below
- metrics: float32 [9, 32, 16, 256], P(None, ('blocks', 'split', 'inner')), may hold values from -1 to 1
- inv_volume: float32 [32, 16, 256], P(('blocks', 'split', 'inner')), may hold values from 0.5 to 1.5
- iblank: int32 [32, 16, 256], P(('blocks', 'split', 'inner')), may hold values 0 or 1
- donor_cells: int32 [16, 8, 256], P(('blocks', 'split', 'inner')), may hold values from 0 to 8191, as said below
- donor_fracs: float32 [16, 3, 256], P(('blocks', 'split', 'inner')), may hold values from 0 to 1
- receiver_cells: int32 [16, 256], P(('blocks', 'split', 'inner')), may hold values from 0 to 8192, as said below
Outputs:
- new_state: float32 [5, 64, 16, 256], P(None, ('cases', 'blocks', 'split', 'inner')), parts along dimension 1
The draws below stay inside these ranges and needn't reach their ends.
There are 2 independent parts, one for each index of `cases`. The reference program is written for one: setup_inputs(seed, part) draws one part's arguments, and reference() takes and returns one part's arrays. A program takes and returns all parts, laid end to end along the dimension named above; an argument that names none is the same for every part. Nothing has to cross between parts.
Inputs may be any that keep to these rules, and one draw needn't show every extreme that they name: `state`: density and pressure are positive; the gas has a ratio of specific heats of 1.4. `donor_cells`: each slot's eight entries are the corners of one hexahedron of the owner's cells: entry c lies at offsets (c // 4, (c // 2) % 2, c % 2) along the three dimensions from entry 0. Slot r * 16 + q serves receiving device r. `receiver_cells`: on each receiving device the entries below 8192 are distinct cells; an entry equal to 8192 is an unused slot. Among the 16 slots from one owner, the used ones come first.
All inputs are finite; a program needn't handle non-finite values. No bound on the sum of `iblank` on one device may be relied on, other than what follows from the above.
Results may differ from the reference program's by a relative error of at most 0.00002.
Values sent between devices are 32-bit elements; how exact they have to be, the bound alone decides.
A program may use at most 64 MiB of HBM per device.

```python
import math
import jax
import jax.numpy as jnp
from jax import lax

NVAR = 5
CX = 2
CY = 16
CZ = 256
CAP = 16
NDEV = 16
NX = 32
BLOCK_X = 8
CELLS = 8192
SLOTS = 256
N_BLOCKS = 4


def draw_state(key, part):
    key = jax.random.fold_in(key, 1)
    subkeys = jax.random.split(key, 3)
    grid_shape = (NX, CY, CZ)
    density = jnp.exp(jax.random.uniform(subkeys[0], grid_shape, jnp.float32, -0.2, 0.2))
    velocity = jnp.clip(0.3 * jax.random.normal(subkeys[1], (3,) + grid_shape, jnp.float32), -0.9, 0.9)
    pressure = jnp.exp(jax.random.uniform(subkeys[2], grid_shape, jnp.float32, -0.2, 0.2)) / 1.4
    momentum = density[None] * velocity
    energy = pressure / 0.4 + 0.5 * density * jnp.sum(velocity * velocity, axis=0)
    return jnp.concatenate([density[None], momentum, energy[None]], axis=0).astype(jnp.float32)


def draw_donor_cells(key, part):
    key = jax.random.fold_in(key, 2)
    subkeys = jax.random.split(key, 3)
    grid_shape = (NDEV, SLOTS)
    slot_index = jnp.arange(SLOTS)[None, :]
    first_index = jax.random.randint(subkeys[0], grid_shape, 0, CX - 1)
    second_index = jax.random.randint(subkeys[1], grid_shape, 0, CY - 1)
    third_index = jax.random.randint(subkeys[2], grid_shape, 0, CZ - 1)
    first_index = jnp.where(slot_index == 0, CX - 2, jnp.where(slot_index == 1, 0, first_index))
    second_index = jnp.where(slot_index == 0, CY - 2, jnp.where(slot_index == 1, 0, second_index))
    third_index = jnp.where(slot_index == 0, CZ - 2, jnp.where(slot_index == 1, 0, third_index))
    stacked = []
    for corner in range(8):
        stacked.append(((first_index + corner // 4) * CY + second_index + corner // 2 % 2) * CZ + third_index + corner % 2)
    return jnp.stack(stacked, axis=1).astype(jnp.int32)


def draw_receiver_cells(key, part):
    key = jax.random.fold_in(key, 3)
    subkeys = jax.random.split(key, 5)
    shuffled = jax.vmap(lambda single: jax.random.permutation(single, CELLS))(jax.random.split(subkeys[0], NDEV))[:, :SLOTS]
    ceiling = jax.random.randint(subkeys[1], (NDEV, 1), 1, CAP + 1)
    counts = jax.random.randint(subkeys[2], (NDEV, NDEV), ceiling // 2, ceiling + 1)
    busiest = jax.random.randint(subkeys[3], (), 0, NDEV)
    empty_owner = jax.random.randint(subkeys[4], (), 0, NDEV)
    row_index = jnp.arange(NDEV)[:, None]
    owner_index = jnp.arange(NDEV)[None, :]
    counts = jnp.where(row_index == busiest, CAP, counts)
    counts = jnp.where(jnp.logical_and(row_index == (busiest + 1) % NDEV, owner_index == empty_owner), 0, counts)
    live_slot = jnp.arange(CAP)[None, None, :] < counts[:, :, None]
    return jnp.where(live_slot.reshape(NDEV, SLOTS), shuffled, CELLS).astype(jnp.int32)


def plant(entries, stream_key, least, high):
    extent = entries.shape
    place = [jax.random.randint(jax.random.fold_in(stream_key, axis), (), 0, extent[axis]) for axis in range(len(extent))]
    entries = entries.at[tuple(place)].set(least)
    longest = extent.index(max(extent))
    place[longest] = (place[longest] + 1) % extent[longest]
    return entries.at[tuple(place)].set(high)


def levels(key, extent, cuts, low, top_value):
    factor_of = 1.0
    for dim, blocks in cuts:
        steps = jax.random.uniform(jax.random.fold_in(jax.random.fold_in(key, 6), dim), (blocks,), jnp.float32, low / len(cuts), top_value / len(cuts))
        factor_of = factor_of * jnp.repeat(jnp.exp(steps), extent[dim] // blocks).reshape((-1,) + (1,) * (len(extent) - 1 - dim))
    return factor_of


def setup_inputs(seed: int = 0, part: int = 0) -> dict:
    key_list = jax.random.split(jax.random.key(seed), 8)
    part_keys = jax.random.split(jax.random.fold_in(key_list[7], part), 8)
    state = draw_state(jax.random.fold_in(jax.random.fold_in(key_list[7], part), 71), part)
    metrics = jnp.clip(jax.random.uniform(key_list[1], (9, NX, CY, CZ), jnp.float32, -1.0, 1.0) * levels(key_list[1], (9, NX, CY, CZ), ((1, 16),), -0.4, 0.0), -1.0, 1.0)
    inv_volume = jnp.clip(jnp.exp(math.log(1.5) - 1.0986123 * jax.random.uniform(key_list[2], (NX, CY, CZ), jnp.float32) ** levels(key_list[2], (NX, CY, CZ), ((0, 16),), -0.2, 0.2)), 0.5, 1.5)
    iblank = plant((jax.random.randint(key_list[3], (NX, CY, CZ), 0, 10) < 9).astype(jnp.int32), jax.random.fold_in(key_list[3], 1), 0, 1)
    donor_cells = draw_donor_cells(jax.random.fold_in(key_list[7], 71), part)
    donor_fracs = jnp.clip(1.0 * jax.random.uniform(key_list[5], (NDEV, 3, SLOTS), jnp.float32) ** levels(key_list[5], (NDEV, 3, SLOTS), ((0, 16),), -0.2, 0.2), 0.0, 1.0)
    receiver_cells = draw_receiver_cells(jax.random.fold_in(key_list[7], 71), part)
    return dict(state=state, metrics=metrics, inv_volume=inv_volume, iblank=iblank, donor_cells=donor_cells, donor_fracs=donor_fracs, receiver_cells=receiver_cells)


HEAT_RATIO = 1.4
TIME_STEP = 0.08

def edge_padded(field, axis):
    length = field.shape[axis]
    lower = lax.slice_in_dim(field, 0, 1, axis=axis)
    upper = lax.slice_in_dim(field, length - 1, length, axis=axis)
    return jnp.concatenate([lower, field, upper], axis=axis)

def fluxes(state, normal):
    density = state[0]
    momentum = state[1:4]
    energy = state[4]
    velocity = momentum / density
    pressure = (HEAT_RATIO - 1.0) * (energy - 0.5 * lax.optimization_barrier(jnp.sum(momentum * velocity, axis=0)))
    normal_speed = lax.optimization_barrier(jnp.sum(velocity * normal, axis=0))
    face_flux = jnp.stack([density * normal_speed, momentum[0] * normal_speed + pressure * normal[0], momentum[1] * normal_speed + pressure * normal[1], momentum[2] * normal_speed + pressure * normal[2], (energy + pressure) * normal_speed])
    radius = jnp.abs(normal_speed) + jnp.sqrt(HEAT_RATIO * pressure / density * lax.optimization_barrier(jnp.sum(normal * normal, axis=0)))
    return (face_flux, radius)

def face_difference(state_ext, normal_ext, axis):
    face_count = state_ext.shape[axis] - 1
    left_state = lax.slice_in_dim(state_ext, 0, face_count, axis=axis)
    right_state = lax.slice_in_dim(state_ext, 1, face_count + 1, axis=axis)
    normal = 0.5 * (lax.slice_in_dim(normal_ext, 0, face_count, axis=axis) + lax.slice_in_dim(normal_ext, 1, face_count + 1, axis=axis))
    left_flux, left_radius = fluxes(left_state, normal)
    right_flux, right_radius = fluxes(right_state, normal)
    face_flux = 0.5 * (left_flux + right_flux) - 0.5 * jnp.maximum(left_radius, right_radius)[None] * (right_state - left_state)
    return lax.slice_in_dim(face_flux, 1, face_count, axis=axis) - lax.slice_in_dim(face_flux, 0, face_count - 1, axis=axis)

def residual_rate(state, state_ext, normal_ext, metrics, inv_volume):
    summed = face_difference(state_ext, normal_ext, 1)
    summed = summed + face_difference(edge_padded(state, 2), edge_padded(metrics[3:6], 2), 2)
    summed = summed + face_difference(edge_padded(state, 3), edge_padded(metrics[6:9], 3), 3)
    return -inv_volume[None] * summed

def corner_weights(fractions):
    stacked = []
    for corner in range(8):
        factor = jnp.ones_like(fractions[0])
        for direction, offset_bit in ((0, corner // 4), (1, corner // 2 % 2), (2, corner % 2)):
            factor = factor * (fractions[direction] if offset_bit else 1.0 - fractions[direction])
        stacked.append(factor)
    return jnp.stack(stacked)

def reference(state, metrics, inv_volume, iblank, donor_cells, donor_fracs, receiver_cells):
    weights = jax.vmap(corner_weights)(donor_fracs)
    row_index = jnp.arange(NDEV)[:, None]
    fringe = jnp.zeros((NDEV, CELLS), jnp.bool_).at[row_index, receiver_cells].set(True, mode='drop').reshape(NX, CY, CZ)
    update = jnp.logical_and(iblank == 1, jnp.logical_not(fringe))

    def owner_values(owner_flat, stencil, weight):
        return lax.optimization_barrier(jnp.sum(owner_flat[:, stencil] * weight[None], axis=1))

    def fill_fringe(current):
        flattened = current.reshape(NVAR, NDEV, CELLS)
        values = jax.vmap(owner_values, in_axes=(1, 0, 0), out_axes=1)(flattened, donor_cells, weights)
        values = values.reshape(NVAR, NDEV, NDEV, CAP).transpose(0, 2, 1, 3).reshape(NVAR, NDEV, SLOTS)
        return flattened.at[:, row_index, receiver_cells].set(values, mode='drop').reshape(current.shape)

    def split_blocks(field):
        return field.reshape(field.shape[0], N_BLOCKS, BLOCK_X, CY, CZ).transpose(1, 0, 2, 3, 4)
    metric_blocks = split_blocks(metrics)
    volume_blocks = inv_volume.reshape(N_BLOCKS, BLOCK_X, CY, CZ)

    def block_step(operands):
        block_state, block_metric, block_volume = operands
        return block_state + TIME_STEP * residual_rate(block_state, edge_padded(block_state, 1), edge_padded(block_metric[0:3], 1), block_metric, block_volume)

    def advance(current):
        stepped = lax.map(block_step, (split_blocks(current), metric_blocks, volume_blocks))
        return stepped.transpose(1, 0, 2, 3, 4).reshape(current.shape)
    first_fill = fill_fringe(state)
    middle = jnp.where(update[None], advance(first_fill), first_fill)
    second_fill = fill_fringe(middle)
    return jnp.where(update[None], 0.5 * first_fill + 0.5 * advance(second_fill), second_fill)
```

```python
import functools

import jax
import jax.numpy as jnp
from jax import lax
from jax.experimental import pallas as pl
from jax.experimental.pallas import tpu as pltpu
from jax.sharding import PartitionSpec as P

HEAT_RATIO = 1.4
TIME_STEP = 0.08
GROUP = ("blocks", "split", "inner")
LANES = 128
MESH = pl.DeviceIdType.MESH


def split3(x):
    high = x.astype(jnp.bfloat16)
    rest = x - high.astype(jnp.float32)
    middle = rest.astype(jnp.bfloat16)
    low = (rest - middle.astype(jnp.float32)).astype(jnp.bfloat16)
    return high, middle, low


def primitive(u):
    density, m0, m1, m2, energy = u
    inverse = 1.0 / density
    pressure = (HEAT_RATIO - 1.0) * (energy - 0.5 * (m0 * m0 + m1 * m1 + m2 * m2) * inverse)
    sound = jnp.sqrt(HEAT_RATIO * pressure * inverse)
    return (density, m0, m1, m2, energy, inverse, pressure, sound)


def face(left, right, normal):
    n0, n1, n2, length = normal
    dl, al, bl, cl, el, il, pl_, sl = left
    dr, ar, br, cr, er, ir, pr, sr = right
    flow_l = al * n0 + bl * n1 + cl * n2
    flow_r = ar * n0 + br * n1 + cr * n2
    wl = flow_l * il
    wr = flow_r * ir
    radius = jnp.maximum(jnp.abs(wl) + sl * length, jnp.abs(wr) + sr * length)
    both = pl_ + pr
    return (
        flow_l + flow_r - radius * (dr - dl),
        al * wl + ar * wr + both * n0 - radius * (ar - al),
        bl * wl + br * wr + both * n1 - radius * (br - bl),
        cl * wl + cr * wr + both * n2 - radius * (cr - cl),
        (el + pl_) * wl + (er + pr) * wr - radius * (er - el),
    )


def twice_flux(cell, normal):
    n0, n1, n2 = (2.0 * n for n in normal)
    _, a, b, c, e, inverse, p, _ = cell
    flow = a * n0 + b * n1 + c * n2
    w = flow * inverse
    return (flow, a * w + p * n0, b * w + p * n1, c * w + p * n2, (e + p) * w)


def next_along(x, axis):
    size = x.shape[axis]
    index = lax.broadcasted_iota(jnp.int32, x.shape, axis)
    return jnp.where(index == size - 1, x, pltpu.roll(x, size - 1, axis))


def averaged(first, second):
    n = tuple(0.5 * (a + b) for a, b in zip(first, second))
    return n + (jnp.sqrt(n[0] * n[0] + n[1] * n[1] + n[2] * n[2]),)


def difference_along(cell, upper_normal, own_normal, axis):
    upper = face(cell, tuple(next_along(x, axis) for x in cell), upper_normal)
    span = 8 if axis == 0 else LANES
    cut = functools.partial(lax.slice_in_dim, start_index=0, limit_index=span, axis=axis)
    ghost = twice_flux(tuple(cut(x) for x in cell), tuple(cut(x) for x in own_normal))
    out = []
    for value, edge in zip(upper, ghost):
        lower = pltpu.roll(value, 1, axis)
        index = lax.broadcasted_iota(jnp.int32, edge.shape, axis)
        first = jnp.where(index == 0, edge, cut(lower))
        rest = lax.slice_in_dim(lower, span, lower.shape[axis], axis=axis)
        out.append(value - jnp.concatenate([first, rest], axis=axis))
    return out


def kernel(
    sizes,
    state_hbm, metrics_hbm, volume_hbm, blank_hbm, cells_hbm, fracs_hbm, targets_hbm,
    out_ref,
    state, metrics, volume, blank, cells, fracs, targets,
    hot, spread, send, recv, halo, halo_metrics, halo_targets, filled, middle, normals, marks,
    load_sem, send_sem, recv_sem, halo_send, halo_recv, once_send, once_recv,
):
    blocks, splits, inners = sizes
    n = blocks * splits * inners
    line = splits * inners
    nvar, planes, columns, depth = state.shape
    slots = targets.shape[1]
    cap = slots // n
    per = LANES // cap
    tiles = slots // LANES

    place = lax.axis_index("split") * inners + lax.axis_index("inner")
    me = lax.axis_index("blocks") * line + place
    has_left = place > 0
    has_right = place < line - 1

    def peer(r):
        return {"blocks": r // line, "split": (r // inners) % splits, "inner": r % inners}

    def beside(step):
        q = place + step
        return {"split": q // inners, "inner": q % inners}

    loads = [
        pltpu.make_async_copy(src, dst, load_sem.at[i])
        for i, (src, dst) in enumerate(
            (
                (cells_hbm, cells), (fracs_hbm, fracs), (state_hbm, state), (targets_hbm, targets),
                (metrics_hbm, metrics), (volume_hbm, volume), (blank_hbm, blank),
            )
        )
    ]
    for load in loads:
        load.start()
    barrier = pltpu.get_barrier_semaphore()
    for d in range(1, n):
        pl.semaphore_signal(
            barrier, inc=1, device_id=peer(lax.rem(me + d, n)), device_id_type=MESH
        )

    def row_of(index, length):
        return lax.broadcasted_iota(jnp.int32, (length, slots), 0) == index

    def one_hot(index, length):
        return jnp.where(row_of(index, length), 1.0, 0.0)

    loads[0].wait()
    loads[1].wait()
    corner = cells[0, 0:1, :]
    k0 = corner % depth
    j0 = (corner // depth) % columns
    i0 = corner // (depth * columns)
    f0, f1, f2 = (fracs[0, g : g + 1, :] for g in range(3))
    hot[:, 0:slots] = one_hot(k0, depth).astype(jnp.bfloat16)
    hot[:, slots : 2 * slots] = one_hot(k0 + 1, depth).astype(jnp.bfloat16)
    weight_j = one_hot(j0, columns) * (1.0 - f1) + one_hot(j0 + 1, columns) * f1
    weight_i = [
        jnp.where(i0 == i, 1.0 - f0, 0.0) + jnp.where(i0 + 1 == i, f0, 0.0)
        for i in range(planes)
    ]
    for i in range(planes):
        marks[i] = weight_j * weight_i[i]

    def gather(source, step):
        rows = nvar * planes * columns
        flat = source[...].reshape(rows, depth)
        parts = split3(flat)
        picked = sum(
            jnp.dot(part, hot[...], preferred_element_type=jnp.float32) for part in parts[::-1]
        )
        along = picked[:, 0:slots] * (1.0 - f2) + picked[:, slots : 2 * slots] * f2
        along = along.reshape(nvar, planes, columns, slots)
        for v in range(nvar):
            total = along[v, 0] * marks[0]
            for i in range(1, planes):
                total = total + along[v, i] * marks[i]
            row = jnp.sum(total, axis=0, keepdims=True)
            for h in range(tiles):
                send[step, h, v : v + 1, :] = row[:, h * LANES : (h + 1) * LANES]

    def exchange(step):
        copies = []
        for d in range(1, n):
            r = lax.rem(me + d, n)
            copies.append(
                pltpu.make_async_remote_copy(
                    src_ref=send.at[step, r // per],
                    dst_ref=recv.at[step, me],
                    send_sem=send_sem.at[step],
                    recv_sem=recv_sem.at[step],
                    device_id=peer(r),
                    device_id_type=MESH,
                )
            )
        for copy in copies:
            copy.start()
        recv[step, me] = send[step, me // per]

    def drain(step, sem):
        pltpu.make_async_copy(
            recv.at[step, pl.ds(0, n - 1)], recv.at[step, pl.ds(0, n - 1)], sem.at[step]
        ).wait()

    def halo_copies(source, step):
        return [
            pltpu.make_async_remote_copy(
                src_ref=source.at[:, 0 if side else planes - 1],
                dst_ref=halo.at[step, side],
                send_sem=halo_send.at[step, side],
                recv_sem=halo_recv.at[step, side],
                device_id=beside(-1 if side else 1),
                device_id_type=MESH,
            )
            for side in range(2)
        ]

    def once_copies():
        out = []
        for side in range(2):
            for item, (src, dst) in enumerate(
                (
                    (targets, halo_targets.at[side]),
                    (metrics.at[pl.ds(0, 3), 0 if side else planes - 1], halo_metrics.at[side]),
                )
            ):
                out.append(
                    pltpu.make_async_remote_copy(
                        src_ref=src,
                        dst_ref=dst,
                        send_sem=once_send.at[side, item],
                        recv_sem=once_recv.at[side, item],
                        device_id=beside(-1 if side else 1),
                        device_id_type=MESH,
                    )
                )
        return out[:2], out[2:]

    def both_sides(pairs, act):
        for side, sends in ((0, has_right), (1, has_left)):

            @pl.when(sends if act in ("start", "wait_send") else (has_left, has_right)[side])
            def _():
                for copy in pairs[side]:
                    getattr(copy, act)()

    loads[2].wait()
    gather(state, 0)
    for load in loads[3:5]:
        load.wait()
    pl.semaphore_wait(barrier, n - 1)
    exchange(0)
    once = once_copies()
    halo_0 = [[copy] for copy in halo_copies(state, 0)]
    both_sides(halo_0, "start")
    both_sides(once, "start")

    for i in range(planes):
        for g in (1, 2):
            own = tuple(metrics[3 * g + x, i] for x in range(3))
            mean = averaged(own, tuple(next_along(x, g - 1) for x in own))
            for x in range(4):
                normals[g, i, x] = mean[x]

    def spread_of(index, cell):
        spread[index] = one_hot(cell % depth, depth).astype(jnp.bfloat16)

    spread_of(0, targets[...])
    for load in loads[5:]:
        load.wait()
    both_sides(once, "wait_recv")
    for side in range(2):
        spread_of(1 + side, halo_targets[side])
    place_rows = [
        targets[...] // depth,
        halo_targets[0] // depth - (planes - 1) * columns,
        halo_targets[1] // depth,
    ]
    rows_of = [planes * columns, columns, columns]
    nt = (((1,), (1,)), ((), ()))
    fringe = []
    for t in range(3):
        found = lax.dot_general(
            one_hot(place_rows[t], rows_of[t]).astype(jnp.bfloat16), spread[t], nt,
            preferred_element_type=jnp.float32,
        )
        fringe.append(found > 0.5)

    first = [metrics[x, 0] for x in range(3)]
    last = [metrics[x, planes - 1] for x in range(3)]
    line_normals = [
        tuple(jnp.where(has_left, halo_metrics[0, x], first[x]) for x in range(3))
    ]
    for i in range(planes):
        line_normals.append(tuple(metrics[x, i] for x in range(3)))
    line_normals.append(
        tuple(jnp.where(has_right, halo_metrics[1, x], last[x]) for x in range(3))
    )
    for i in range(planes + 1):
        mean = averaged(line_normals[i], line_normals[i + 1])
        for x in range(4):
            normals[0, i, x] = mean[x]

    segment = lax.broadcasted_iota(jnp.int32, (8, LANES), 1) // cap

    def arrived(step):
        whole = [[], [], []]
        for h in range(tiles):
            sums = [jnp.zeros((8, LANES), jnp.float32)] * 3
            for o in range(h * per, (h + 1) * per):
                tile = pltpu.roll(recv[step, o], lax.rem(o - me + n * per, per) * cap, 1)
                for t, shift in enumerate((0, -1, 1)):
                    sums[t] = jnp.where(segment == (o + shift) % per, tile, sums[t])
            whole[0].append(sums[0])
            whole[1].append(pltpu.roll(sums[1], cap, 1))
            whole[2].append(pltpu.roll(sums[2], LANES - cap, 1))
        return [jnp.concatenate(w, axis=1) for w in whole]

    def fill(step, t, values, current):
        mine = row_of(place_rows[t], rows_of[t])
        parts = []
        for part in split3(values):
            wide = part.astype(jnp.float32)
            parts.append(
                jnp.concatenate(
                    [jnp.where(mine, wide[v : v + 1, :], 0.0) for v in range(nvar)], axis=0
                ).astype(jnp.bfloat16)
            )
        placed = sum(
            lax.dot_general(part, spread[t], nt, preferred_element_type=jnp.float32)
            for part in parts[::-1]
        )
        out = []
        for i, plane in enumerate(current):
            at = slice(i * columns, (i + 1) * columns)
            out.append(
                [
                    jnp.where(
                        fringe[t][at],
                        placed[v * rows_of[t] + i * columns : v * rows_of[t] + (i + 1) * columns],
                        plane[v],
                    )
                    for v in range(nvar)
                ]
            )
        return out

    def planes_of(ref):
        return [[ref[v, i] for v in range(nvar)] for i in range(planes)]

    def section(step, source, halo_pairs):
        drain(step, recv_sem)
        values = arrived(step)
        own = fill(step, 0, values[0], planes_of(source))
        for i in range(planes):
            for v in range(nvar):
                filled[step, v, i] = own[i][v]
        both_sides(halo_pairs, "wait_recv")
        left = fill(step, 1, values[1], [[halo[step, 0, v] for v in range(nvar)]])[0]
        right = fill(step, 2, values[2], [[halo[step, 1, v] for v in range(nvar)]])[0]
        left = [jnp.where(has_left, a, b) for a, b in zip(left, own[0])]
        right = [jnp.where(has_right, a, b) for a, b in zip(right, own[planes - 1])]
        cell = [primitive(u) for u in [left] + own + [right]]
        faces = [
            face(cell[i], cell[i + 1], tuple(normals[0, i, x] for x in range(4)))
            for i in range(planes + 1)
        ]
        stepped = []
        for i in range(planes):
            total = [b - a for a, b in zip(faces[i], faces[i + 1])]
            for g in (1, 2):
                more = difference_along(
                    cell[i + 1],
                    tuple(normals[g, i, x] for x in range(4)),
                    tuple(metrics[3 * g + x, i] for x in range(3)),
                    g - 1,
                )
                total = [a + b for a, b in zip(total, more)]
            factor = (-0.5 * TIME_STEP) * volume[i]
            update = jnp.logical_and(
                blank[i] == 1, jnp.logical_not(fringe[0][i * columns : (i + 1) * columns])
            )
            stepped.append((update, [factor * x for x in total]))
        return stepped

    for i, (update, change) in enumerate(section(0, state, halo_0)):
        for v in range(nvar):
            middle[v, i] = filled[0, v, i] + jnp.where(update, change[v], 0.0)
    halo_1 = [[copy] for copy in halo_copies(middle, 1)]
    both_sides(halo_1, "start")
    gather(middle, 1)
    exchange(1)
    for i, (update, change) in enumerate(section(1, middle, halo_1)):
        for v in range(nvar):
            end = filled[1, v, i]
            out_ref[v, i] = jnp.where(
                update, 0.5 * filled[0, v, i] + 0.5 * (end + change[v]), end
            )
    for step in range(2):
        drain(step, send_sem)
    for pairs in (halo_0, halo_1, once):
        both_sides(pairs, "wait_send")


def local(sizes, state, metrics, inv_volume, iblank, donor_cells, donor_fracs, receiver_cells):
    nvar, planes, columns, depth = state.shape
    slots = receiver_cells.shape[1]
    n = sizes[0] * sizes[1] * sizes[2]
    tiles = slots // LANES
    f32, bf16, i32 = jnp.float32, jnp.bfloat16, jnp.int32
    dma = pltpu.SemaphoreType.DMA
    return pl.pallas_call(
        functools.partial(kernel, sizes),
        out_shape=jax.ShapeDtypeStruct(state.shape, f32),
        in_specs=[pl.BlockSpec(memory_space=pl.ANY)] * 7,
        out_specs=pl.BlockSpec(memory_space=pltpu.VMEM),
        scratch_shapes=[
            pltpu.VMEM(state.shape, f32),
            pltpu.VMEM(metrics.shape, f32),
            pltpu.VMEM(inv_volume.shape, f32),
            pltpu.VMEM(iblank.shape, i32),
            pltpu.VMEM(donor_cells.shape, i32),
            pltpu.VMEM(donor_fracs.shape, f32),
            pltpu.VMEM(receiver_cells.shape, i32),
            pltpu.VMEM((depth, 2 * slots), bf16),
            pltpu.VMEM((3, depth, slots), bf16),
            pltpu.VMEM((2, tiles, 8, LANES), f32),
            pltpu.VMEM((2, n, 8, LANES), f32),
            pltpu.VMEM((2, 2, nvar, columns, depth), f32),
            pltpu.VMEM((2, 3, columns, depth), f32),
            pltpu.VMEM((2, 1, slots), i32),
            pltpu.VMEM((2,) + state.shape, f32),
            pltpu.VMEM(state.shape, f32),
            pltpu.VMEM((3, planes + 1, 4, columns, depth), f32),
            pltpu.VMEM((planes, columns, slots), f32),
            dma((7,)),
            dma((2,)),
            dma((2,)),
            dma((2, 2)),
            dma((2, 2)),
            dma((2, 2)),
            dma((2, 2)),
        ],
        compiler_params=pltpu.CompilerParams(
            collective_id=0, has_side_effects=True, vmem_limit_bytes=40 * 1024 * 1024
        ),
    )(state, metrics, inv_volume, iblank, donor_cells, donor_fracs, receiver_cells)


def solution(mesh):
    sizes = tuple(mesh.shape[axis] for axis in GROUP)
    return jax.shard_map(
        functools.partial(local, sizes),
        mesh=mesh,
        in_specs=(
            P(None, ("cases", "blocks", "split", "inner"), None, None),
            P(None, ("blocks", "split", "inner"), None, None),
            P(("blocks", "split", "inner"), None, None),
            P(("blocks", "split", "inner"), None, None),
            P(("blocks", "split", "inner"), None, None),
            P(("blocks", "split", "inner"), None, None),
            P(("blocks", "split", "inner"), None),
        ),
        out_specs=P(None, ("cases", "blocks", "split", "inner"), None, None),
        check_vma=False,
    )
```

```python
import functools

import jax
import jax.numpy as jnp
from jax import lax
from jax.experimental import pallas as pl
from jax.experimental.pallas import tpu as pltpu
from jax.sharding import PartitionSpec as P

HEAT_RATIO = 1.4
TIME_STEP = 0.08
GROUP = ("blocks", "split", "inner")
LANES = 128
MESH = pl.DeviceIdType.MESH


def split3(x):
    high = x.astype(jnp.bfloat16)
    rest = x - high.astype(jnp.float32)
    middle = rest.astype(jnp.bfloat16)
    low = (rest - middle.astype(jnp.float32)).astype(jnp.bfloat16)
    return high, middle, low


def primitive(u):
    density, m0, m1, m2, energy = u
    inverse = 1.0 / density
    pressure = (HEAT_RATIO - 1.0) * (energy - 0.5 * (m0 * m0 + m1 * m1 + m2 * m2) * inverse)
    sound = jnp.sqrt(HEAT_RATIO * pressure * inverse)
    return (density, m0, m1, m2, energy, inverse, pressure, sound)


def face(left, right, normal):
    n0, n1, n2, length = normal
    dl, al, bl, cl, el, il, pl_, sl = left
    dr, ar, br, cr, er, ir, pr, sr = right
    flow_l = al * n0 + bl * n1 + cl * n2
    flow_r = ar * n0 + br * n1 + cr * n2
    wl = flow_l * il
    wr = flow_r * ir
    radius = jnp.maximum(jnp.abs(wl) + sl * length, jnp.abs(wr) + sr * length)
    both = pl_ + pr
    return (
        flow_l + flow_r - radius * (dr - dl),
        al * wl + ar * wr + both * n0 - radius * (ar - al),
        bl * wl + br * wr + both * n1 - radius * (br - bl),
        cl * wl + cr * wr + both * n2 - radius * (cr - cl),
        (el + pl_) * wl + (er + pr) * wr - radius * (er - el),
    )


def twice_flux(cell, normal):
    n0, n1, n2 = (2.0 * n for n in normal)
    _, a, b, c, e, inverse, p, _ = cell
    flow = a * n0 + b * n1 + c * n2
    w = flow * inverse
    return (flow, a * w + p * n0, b * w + p * n1, c * w + p * n2, (e + p) * w)


def next_along(x, axis):
    size = x.shape[axis]
    index = lax.broadcasted_iota(jnp.int32, x.shape, axis)
    return jnp.where(index == size - 1, x, pltpu.roll(x, size - 1, axis))


def averaged(first, second):
    n = tuple(0.5 * (a + b) for a, b in zip(first, second))
    return n + (jnp.sqrt(n[0] * n[0] + n[1] * n[1] + n[2] * n[2]),)


def difference_along(cell, upper_normal, own_normal, axis):
    upper = face(cell, tuple(next_along(x, axis) for x in cell), upper_normal)
    span = 8 if axis == 0 else LANES
    cut = functools.partial(lax.slice_in_dim, start_index=0, limit_index=span, axis=axis)
    ghost = twice_flux(tuple(cut(x) for x in cell), tuple(cut(x) for x in own_normal))
    out = []
    for value, edge in zip(upper, ghost):
        lower = pltpu.roll(value, 1, axis)
        index = lax.broadcasted_iota(jnp.int32, edge.shape, axis)
        first = jnp.where(index == 0, edge, cut(lower))
        rest = lax.slice_in_dim(lower, span, lower.shape[axis], axis=axis)
        out.append(value - jnp.concatenate([first, rest], axis=axis))
    return out


def kernel(
    sizes,
    state_hbm, metrics_hbm, volume_hbm, blank_hbm, cells_hbm, fracs_hbm, targets_hbm,
    out_ref,
    state, metrics, volume, blank, cells, fracs, targets,
    hot, spread, send, recv, halo, halo_metrics, halo_targets, filled, middle, normals, marks,
    load_sem, send_sem, recv_sem, halo_send, halo_recv, once_send, once_recv,
):
    blocks, splits, inners = sizes
    n = blocks * splits * inners
    line = splits * inners
    nvar, planes, columns, depth = state.shape
    slots = targets.shape[1]
    cap = slots // n
    per = LANES // cap
    tiles = slots // LANES

    place = lax.axis_index("split") * inners + lax.axis_index("inner")
    me = lax.axis_index("blocks") * line + place
    has_left = place > 0
    has_right = place < line - 1

    def peer(r):
        return {"blocks": r // line, "split": (r // inners) % splits, "inner": r % inners}

    def beside(step):
        q = place + step
        return {"split": q // inners, "inner": q % inners}

    loads = [
        pltpu.make_async_copy(src, dst, load_sem.at[i])
        for i, (src, dst) in enumerate(
            (
                (cells_hbm, cells), (fracs_hbm, fracs), (state_hbm, state), (targets_hbm, targets),
                (metrics_hbm, metrics), (volume_hbm, volume), (blank_hbm, blank),
            )
        )
    ]
    for load in loads:
        load.start()
    barrier = pltpu.get_barrier_semaphore()
    for d in range(1, n):
        pl.semaphore_signal(
            barrier, inc=1, device_id=peer(lax.rem(me + d, n)), device_id_type=MESH
        )

    def row_of(index, length):
        return lax.broadcasted_iota(jnp.int32, (length, slots), 0) == index

    def one_hot(index, length):
        return jnp.where(row_of(index, length), 1.0, 0.0)

    loads[0].wait()
    loads[1].wait()
    corner = cells[0, 0:1, :]
    k0 = corner % depth
    j0 = (corner // depth) % columns
    i0 = corner // (depth * columns)
    f0, f1, f2 = (fracs[g] for g in range(3))
    hot[:, 0:slots] = one_hot(k0, depth).astype(jnp.bfloat16)
    hot[:, slots : 2 * slots] = one_hot(k0 + 1, depth).astype(jnp.bfloat16)
    weight_j = one_hot(j0, columns) * (1.0 - f1) + one_hot(j0 + 1, columns) * f1
    weight_i = [
        jnp.where(i0 == i, 1.0 - f0, 0.0) + jnp.where(i0 + 1 == i, f0, 0.0)
        for i in range(planes)
    ]
    for i in range(planes):
        marks[i] = weight_j * weight_i[i]

    def gather(source, step):
        rows = nvar * planes * columns
        flat = source[...].reshape(rows, depth)
        parts = split3(flat)
        picked = sum(
            jnp.dot(part, hot[...], preferred_element_type=jnp.float32) for part in parts[::-1]
        )
        along = picked[:, 0:slots] * (1.0 - f2) + picked[:, slots : 2 * slots] * f2
        along = along.reshape(nvar, planes, columns, slots)
        for v in range(nvar):
            total = along[v, 0] * marks[0]
            for i in range(1, planes):
                total = total + along[v, i] * marks[i]
            row = jnp.sum(total, axis=0, keepdims=True)
            for h in range(tiles):
                send[step, h, v : v + 1, :] = row[:, h * LANES : (h + 1) * LANES]

    def exchange(step):
        copies = []
        for d in range(1, n):
            r = lax.rem(me + d, n)
            copies.append(
                pltpu.make_async_remote_copy(
                    src_ref=send.at[step, r // per],
                    dst_ref=recv.at[step, me],
                    send_sem=send_sem.at[step],
                    recv_sem=recv_sem.at[step],
                    device_id=peer(r),
                    device_id_type=MESH,
                )
            )
        for copy in copies:
            copy.start()
        recv[step, me] = send[step, me // per]

    def drain(step, sem):
        pltpu.make_async_copy(
            recv.at[step, pl.ds(0, n - 1)], recv.at[step, pl.ds(0, n - 1)], sem.at[step]
        ).wait()

    def halo_copies(source, step):
        return [
            pltpu.make_async_remote_copy(
                src_ref=source.at[:, 0 if side else planes - 1],
                dst_ref=halo.at[step, side],
                send_sem=halo_send.at[step, side],
                recv_sem=halo_recv.at[step, side],
                device_id=beside(-1 if side else 1),
                device_id_type=MESH,
            )
            for side in range(2)
        ]

    def once_copies():
        out = []
        for side in range(2):
            for item, (src, dst) in enumerate(
                (
                    (targets, halo_targets.at[side]),
                    (metrics.at[pl.ds(0, 3), 0 if side else planes - 1], halo_metrics.at[side]),
                )
            ):
                out.append(
                    pltpu.make_async_remote_copy(
                        src_ref=src,
                        dst_ref=dst,
                        send_sem=once_send.at[side, item],
                        recv_sem=once_recv.at[side, item],
                        device_id=beside(-1 if side else 1),
                        device_id_type=MESH,
                    )
                )
        return out[:2], out[2:]

    def both_sides(pairs, act):
        for side, sends in ((0, has_right), (1, has_left)):

            @pl.when(sends if act in ("start", "wait_send") else (has_left, has_right)[side])
            def _():
                for copy in pairs[side]:
                    getattr(copy, act)()

    loads[2].wait()
    gather(state, 0)
    for load in loads[3:5]:
        load.wait()
    pl.semaphore_wait(barrier, n - 1)
    exchange(0)
    once = once_copies()
    halo_0 = [[copy] for copy in halo_copies(state, 0)]
    both_sides(halo_0, "start")
    both_sides(once, "start")

    for i in range(planes):
        for g in (1, 2):
            own = tuple(metrics[3 * g + x, i] for x in range(3))
            mean = averaged(own, tuple(next_along(x, g - 1) for x in own))
            for x in range(4):
                normals[g, i, x] = mean[x]

    def spread_of(index, cell):
        spread[index] = one_hot(cell % depth, depth).astype(jnp.bfloat16)

    spread_of(0, targets[...])
    for load in loads[5:]:
        load.wait()
    both_sides(once, "wait_recv")
    for side in range(2):
        spread_of(1 + side, halo_targets[side])
    place_rows = [
        targets[...] // depth,
        halo_targets[0] // depth - (planes - 1) * columns,
        halo_targets[1] // depth,
    ]
    rows_of = [planes * columns, columns, columns]
    nt = (((1,), (1,)), ((), ()))
    fringe = []
    for t in range(3):
        found = lax.dot_general(
            one_hot(place_rows[t], rows_of[t]).astype(jnp.bfloat16), spread[t], nt,
            preferred_element_type=jnp.float32,
        )
        fringe.append(found > 0.5)

    first = [metrics[x, 0] for x in range(3)]
    last = [metrics[x, planes - 1] for x in range(3)]
    line_normals = [
        tuple(jnp.where(has_left, halo_metrics[0, x], first[x]) for x in range(3))
    ]
    for i in range(planes):
        line_normals.append(tuple(metrics[x, i] for x in range(3)))
    line_normals.append(
        tuple(jnp.where(has_right, halo_metrics[1, x], last[x]) for x in range(3))
    )
    for i in range(planes + 1):
        mean = averaged(line_normals[i], line_normals[i + 1])
        for x in range(4):
            normals[0, i, x] = mean[x]

    segment = lax.broadcasted_iota(jnp.int32, (8, LANES), 1) // cap

    def arrived(step):
        whole = [[], [], []]
        for h in range(tiles):
            sums = [jnp.zeros((8, LANES), jnp.float32)] * 3
            for o in range(h * per, (h + 1) * per):
                tile = pltpu.roll(recv[step, o], lax.rem(o - me + n * per, per) * cap, 1)
                for t, shift in enumerate((0, -1, 1)):
                    sums[t] = jnp.where(segment == (o + shift) % per, tile, sums[t])
            whole[0].append(sums[0])
            whole[1].append(pltpu.roll(sums[1], cap, 1))
            whole[2].append(pltpu.roll(sums[2], LANES - cap, 1))
        return [jnp.concatenate(w, axis=1) for w in whole]

    def fill(step, t, values, current):
        mine = row_of(place_rows[t], rows_of[t])
        parts = []
        for part in split3(values):
            wide = part.astype(jnp.float32)
            parts.append(
                jnp.concatenate(
                    [jnp.where(mine, wide[v : v + 1, :], 0.0) for v in range(nvar)], axis=0
                ).astype(jnp.bfloat16)
            )
        placed = sum(
            lax.dot_general(part, spread[t], nt, preferred_element_type=jnp.float32)
            for part in parts[::-1]
        )
        out = []
        for i, plane in enumerate(current):
            at = slice(i * columns, (i + 1) * columns)
            out.append(
                [
                    jnp.where(
                        fringe[t][at],
                        placed[v * rows_of[t] + i * columns : v * rows_of[t] + (i + 1) * columns],
                        plane[v],
                    )
                    for v in range(nvar)
                ]
            )
        return out

    def planes_of(ref):
        return [[ref[v, i] for v in range(nvar)] for i in range(planes)]

    def section(step, source, halo_pairs):
        drain(step, recv_sem)
        values = arrived(step)
        own = fill(step, 0, values[0], planes_of(source))
        for i in range(planes):
            for v in range(nvar):
                filled[step, v, i] = own[i][v]
        both_sides(halo_pairs, "wait_recv")
        left = fill(step, 1, values[1], [[halo[step, 0, v] for v in range(nvar)]])[0]
        right = fill(step, 2, values[2], [[halo[step, 1, v] for v in range(nvar)]])[0]
        left = [jnp.where(has_left, a, b) for a, b in zip(left, own[0])]
        right = [jnp.where(has_right, a, b) for a, b in zip(right, own[planes - 1])]
        cell = [primitive(u) for u in [left] + own + [right]]
        faces = [
            face(cell[i], cell[i + 1], tuple(normals[0, i, x] for x in range(4)))
            for i in range(planes + 1)
        ]
        stepped = []
        for i in range(planes):
            total = [b - a for a, b in zip(faces[i], faces[i + 1])]
            for g in (1, 2):
                more = difference_along(
                    cell[i + 1],
                    tuple(normals[g, i, x] for x in range(4)),
                    tuple(metrics[3 * g + x, i] for x in range(3)),
                    g - 1,
                )
                total = [a + b for a, b in zip(total, more)]
            factor = (-0.5 * TIME_STEP) * volume[i]
            update = jnp.logical_and(
                blank[i] == 1, jnp.logical_not(fringe[0][i * columns : (i + 1) * columns])
            )
            stepped.append((update, [factor * x for x in total]))
        return stepped

    for i, (update, change) in enumerate(section(0, state, halo_0)):
        for v in range(nvar):
            middle[v, i] = filled[0, v, i] + jnp.where(update, change[v], 0.0)
    halo_1 = [[copy] for copy in halo_copies(middle, 1)]
    both_sides(halo_1, "start")
    gather(middle, 1)
    exchange(1)
    for i, (update, change) in enumerate(section(1, middle, halo_1)):
        for v in range(nvar):
            end = filled[1, v, i]
            out_ref[v, i] = jnp.where(
                update, 0.5 * filled[0, v, i] + 0.5 * (end + change[v]), end
            )
    for step in range(2):
        drain(step, send_sem)
    for pairs in (halo_0, halo_1, once):
        both_sides(pairs, "wait_send")


def local(sizes, state, metrics, inv_volume, iblank, donor_cells, donor_fracs, receiver_cells):
    nvar, planes, columns, depth = state.shape
    slots = receiver_cells.shape[1]
    n = sizes[0] * sizes[1] * sizes[2]
    tiles = slots // LANES
    f32, bf16, i32 = jnp.float32, jnp.bfloat16, jnp.int32
    dma = pltpu.SemaphoreType.DMA
    return pl.pallas_call(
        functools.partial(kernel, sizes),
        out_shape=jax.ShapeDtypeStruct(state.shape, f32),
        in_specs=[pl.BlockSpec(memory_space=pltpu.HBM)] * 7,
        out_specs=pl.BlockSpec(memory_space=pltpu.VMEM),
        scratch_shapes=[
            pltpu.VMEM(state.shape, f32),
            pltpu.VMEM(metrics.shape, f32),
            pltpu.VMEM(inv_volume.shape, f32),
            pltpu.VMEM(iblank.shape, i32),
            pltpu.VMEM(donor_cells.shape, i32),
            pltpu.VMEM((3, 1, slots), f32),
            pltpu.VMEM(receiver_cells.shape, i32),
            pltpu.VMEM((depth, 2 * slots), bf16),
            pltpu.VMEM((3, depth, slots), bf16),
            pltpu.VMEM((2, tiles, 8, LANES), f32),
            pltpu.VMEM((2, n, 8, LANES), f32),
            pltpu.VMEM((2, 2, nvar, columns, depth), f32),
            pltpu.VMEM((2, 3, columns, depth), f32),
            pltpu.VMEM((2, 1, slots), i32),
            pltpu.VMEM((2,) + state.shape, f32),
            pltpu.VMEM(state.shape, f32),
            pltpu.VMEM((3, planes + 1, 4, columns, depth), f32),
            pltpu.VMEM((planes, columns, slots), f32),
            dma((7,)),
            dma((2,)),
            dma((2,)),
            dma((2, 2)),
            dma((2, 2)),
            dma((2, 2)),
            dma((2, 2)),
        ],
        compiler_params=pltpu.CompilerParams(
            collective_id=0, has_side_effects=True, vmem_limit_bytes=40 * 1024 * 1024
        ),
    )(
        *(
            pltpu.with_memory_space_constraint(x, pltpu.HBM)
            for x in (
                state, metrics, inv_volume, iblank, donor_cells,
                donor_fracs.reshape(3, 1, slots), receiver_cells,
            )
        )
    )


def solution(mesh):
    sizes = tuple(mesh.shape[axis] for axis in GROUP)
    return jax.shard_map(
        functools.partial(local, sizes),
        mesh=mesh,
        in_specs=(
            P(None, ("cases", "blocks", "split", "inner"), None, None),
            P(None, ("blocks", "split", "inner"), None, None),
            P(("blocks", "split", "inner"), None, None),
            P(("blocks", "split", "inner"), None, None),
            P(("blocks", "split", "inner"), None, None),
            P(("blocks", "split", "inner"), None, None),
            P(("blocks", "split", "inner"), None),
        ),
        out_specs=P(None, ("cases", "blocks", "split", "inner"), None, None),
        check_vma=False,
    )
```

```python
import functools

import jax
import jax.numpy as jnp
from jax import lax
from jax.experimental import pallas as pl
from jax.experimental.pallas import tpu as pltpu
from jax.sharding import PartitionSpec as P

HEAT_RATIO = 1.4
TIME_STEP = 0.08
GROUP = ("blocks", "split", "inner")
LANES = 128
MESH = pl.DeviceIdType.MESH


def split2(x):
    high = x.astype(jnp.bfloat16)
    rest = x - high.astype(jnp.float32)
    return high, rest.astype(jnp.bfloat16)


def primitive(u):
    density, m0, m1, m2, energy = u
    inverse = 1.0 / density
    pressure = (HEAT_RATIO - 1.0) * (energy - 0.5 * (m0 * m0 + m1 * m1 + m2 * m2) * inverse)
    sound = jnp.sqrt(HEAT_RATIO * pressure * inverse)
    return (density, m0, m1, m2, energy, inverse, pressure, sound)


def face(left, right, normal):
    n0, n1, n2, length = normal
    dl, al, bl, cl, el, il, pl_, sl = left
    dr, ar, br, cr, er, ir, pr, sr = right
    flow_l = al * n0 + bl * n1 + cl * n2
    flow_r = ar * n0 + br * n1 + cr * n2
    wl = flow_l * il
    wr = flow_r * ir
    radius = jnp.maximum(jnp.abs(wl) + sl * length, jnp.abs(wr) + sr * length)
    both = pl_ + pr
    return (
        flow_l + flow_r - radius * (dr - dl),
        al * wl + ar * wr + both * n0 - radius * (ar - al),
        bl * wl + br * wr + both * n1 - radius * (br - bl),
        cl * wl + cr * wr + both * n2 - radius * (cr - cl),
        (el + pl_) * wl + (er + pr) * wr - radius * (er - el),
    )


def twice_flux(cell, normal):
    n0, n1, n2 = (2.0 * n for n in normal)
    _, a, b, c, e, inverse, p, _ = cell
    flow = a * n0 + b * n1 + c * n2
    w = flow * inverse
    return (flow, a * w + p * n0, b * w + p * n1, c * w + p * n2, (e + p) * w)


def next_along(x, axis):
    size = x.shape[axis]
    index = lax.broadcasted_iota(jnp.int32, x.shape, axis)
    return jnp.where(index == size - 1, x, pltpu.roll(x, size - 1, axis))


def averaged(first, second):
    n = tuple(0.5 * (a + b) for a, b in zip(first, second))
    return n + (jnp.sqrt(n[0] * n[0] + n[1] * n[1] + n[2] * n[2]),)


def difference_along(cell, upper_normal, own_normal, axis):
    upper = face(cell, tuple(next_along(x, axis) for x in cell), upper_normal)
    span = 8 if axis == 0 else LANES
    cut = functools.partial(lax.slice_in_dim, start_index=0, limit_index=span, axis=axis)
    ghost = twice_flux(tuple(cut(x) for x in cell), tuple(cut(x) for x in own_normal))
    out = []
    for value, edge in zip(upper, ghost):
        lower = pltpu.roll(value, 1, axis)
        index = lax.broadcasted_iota(jnp.int32, edge.shape, axis)
        first = jnp.where(index == 0, edge, cut(lower))
        rest = lax.slice_in_dim(lower, span, lower.shape[axis], axis=axis)
        out.append(value - jnp.concatenate([first, rest], axis=axis))
    return out


def kernel(
    sizes,
    state_hbm, metrics_hbm, volume_hbm, blank_hbm, cells_hbm, fracs_hbm, targets_hbm,
    out_ref,
    state, metrics, volume, blank, cells, fracs, targets,
    hot, spread, send, recv, halo, halo_metrics, halo_targets, filled, middle, normals, marks,
    load_sem, send_sem, recv_sem, halo_send, halo_recv, once_send, once_recv,
):
    blocks, splits, inners = sizes
    n = blocks * splits * inners
    line = splits * inners
    nvar, planes, columns, depth = state.shape
    slots = targets.shape[1]
    cap = slots // n
    per = LANES // cap
    tiles = slots // LANES

    place = lax.axis_index("split") * inners + lax.axis_index("inner")
    me = lax.axis_index("blocks") * line + place
    has_left = place > 0
    has_right = place < line - 1

    def peer(r):
        return {"blocks": r // line, "split": (r // inners) % splits, "inner": r % inners}

    def beside(step):
        q = place + step
        return {"split": q // inners, "inner": q % inners}

    loads = [
        pltpu.make_async_copy(src, dst, load_sem.at[i])
        for i, (src, dst) in enumerate(
            (
                (cells_hbm, cells), (fracs_hbm, fracs), (state_hbm, state), (targets_hbm, targets),
                (metrics_hbm, metrics), (volume_hbm, volume), (blank_hbm, blank),
            )
        )
    ]
    barrier = pltpu.get_barrier_semaphore()
    for d in range(1, n):
        pl.semaphore_signal(
            barrier, inc=1, device_id=peer(lax.rem(me + d, n)), device_id_type=MESH
        )
    for load in loads:
        load.start()

    def row_of(index, length):
        return lax.broadcasted_iota(jnp.int32, (length, slots), 0) == index

    def one_hot(index, length):
        return jnp.where(row_of(index, length), 1.0, 0.0)

    loads[0].wait()
    loads[1].wait()
    corner = cells[0, 0:1, :]
    k0 = corner % depth
    j0 = (corner // depth) % columns
    i0 = corner // (depth * columns)
    f0, f1, f2 = (fracs[g] for g in range(3))
    hot[:, 0:slots] = one_hot(k0, depth).astype(jnp.bfloat16)
    hot[:, slots : 2 * slots] = one_hot(k0 + 1, depth).astype(jnp.bfloat16)
    weight_j = one_hot(j0, columns) * (1.0 - f1) + one_hot(j0 + 1, columns) * f1
    weight_i = [
        jnp.where(i0 == i, 1.0 - f0, 0.0) + jnp.where(i0 + 1 == i, f0, 0.0)
        for i in range(planes)
    ]
    for i in range(planes):
        marks[i] = weight_j * weight_i[i]

    def gather(source, step):
        rows = nvar * planes * columns
        flat = source[...].reshape(rows, depth)
        parts = split2(flat)
        picked = sum(
            jnp.dot(part, hot[...], preferred_element_type=jnp.float32) for part in parts[::-1]
        )
        along = picked[:, 0:slots] * (1.0 - f2) + picked[:, slots : 2 * slots] * f2
        along = along.reshape(nvar, planes, columns, slots)
        for v in range(nvar):
            total = along[v, 0] * marks[0]
            for i in range(1, planes):
                total = total + along[v, i] * marks[i]
            row = jnp.sum(total, axis=0, keepdims=True)
            for h in range(tiles):
                send[step, h, v : v + 1, :] = row[:, h * LANES : (h + 1) * LANES]

    def exchange(step):
        copies = []
        for d in range(1, n):
            r = lax.rem(me + d, n)
            copies.append(
                pltpu.make_async_remote_copy(
                    src_ref=send.at[step, r // per],
                    dst_ref=recv.at[step, me],
                    send_sem=send_sem.at[step],
                    recv_sem=recv_sem.at[step],
                    device_id=peer(r),
                    device_id_type=MESH,
                )
            )
        for copy in copies:
            copy.start()
        recv[step, me] = send[step, me // per]

    def drain(step, sem):
        pltpu.make_async_copy(
            recv.at[step, pl.ds(0, n - 1)], recv.at[step, pl.ds(0, n - 1)], sem.at[step]
        ).wait()

    def halo_copies(source, step):
        return [
            pltpu.make_async_remote_copy(
                src_ref=source.at[:, 0 if side else planes - 1],
                dst_ref=halo.at[step, side],
                send_sem=halo_send.at[step, side],
                recv_sem=halo_recv.at[step, side],
                device_id=beside(-1 if side else 1),
                device_id_type=MESH,
            )
            for side in range(2)
        ]

    def once_copies():
        out = []
        for side in range(2):
            for item, (src, dst) in enumerate(
                (
                    (targets, halo_targets.at[side]),
                    (metrics.at[pl.ds(0, 3), 0 if side else planes - 1], halo_metrics.at[side]),
                )
            ):
                out.append(
                    pltpu.make_async_remote_copy(
                        src_ref=src,
                        dst_ref=dst,
                        send_sem=once_send.at[side, item],
                        recv_sem=once_recv.at[side, item],
                        device_id=beside(-1 if side else 1),
                        device_id_type=MESH,
                    )
                )
        return out[:2], out[2:]

    def both_sides(pairs, act):
        for side, sends in ((0, has_right), (1, has_left)):

            @pl.when(sends if act in ("start", "wait_send") else (has_left, has_right)[side])
            def _():
                for copy in pairs[side]:
                    getattr(copy, act)()

    loads[2].wait()
    gather(state, 0)
    for load in loads[3:5]:
        load.wait()
    pl.semaphore_wait(barrier, n - 1)
    exchange(0)
    once = once_copies()
    halo_0 = [[copy] for copy in halo_copies(state, 0)]
    both_sides(halo_0, "start")
    both_sides(once, "start")

    for i in range(planes):
        for g in (1, 2):
            own = tuple(metrics[3 * g + x, i] for x in range(3))
            mean = averaged(own, tuple(next_along(x, g - 1) for x in own))
            for x in range(4):
                normals[g, i, x] = mean[x]

    def spread_of(index, cell):
        spread[index] = one_hot(cell % depth, depth).T.astype(jnp.bfloat16)

    spread_of(0, targets[...])
    for load in loads[5:]:
        load.wait()
    both_sides(once, "wait_recv")
    for side in range(2):
        spread_of(1 + side, halo_targets[side])
    place_rows = [
        targets[...] // depth,
        halo_targets[0] // depth - (planes - 1) * columns,
        halo_targets[1] // depth,
    ]
    rows_of = [planes * columns, columns, columns]
    fringe = []
    for t in range(3):
        found = jnp.dot(
            one_hot(place_rows[t], rows_of[t]).astype(jnp.bfloat16), spread[t],
            preferred_element_type=jnp.float32,
        )
        fringe.append(found > 0.5)

    first = [metrics[x, 0] for x in range(3)]
    last = [metrics[x, planes - 1] for x in range(3)]
    line_normals = [
        tuple(jnp.where(has_left, halo_metrics[0, x], first[x]) for x in range(3))
    ]
    for i in range(planes):
        line_normals.append(tuple(metrics[x, i] for x in range(3)))
    line_normals.append(
        tuple(jnp.where(has_right, halo_metrics[1, x], last[x]) for x in range(3))
    )
    for i in range(planes + 1):
        mean = averaged(line_normals[i], line_normals[i + 1])
        for x in range(4):
            normals[0, i, x] = mean[x]

    segment = lax.broadcasted_iota(jnp.int32, (8, LANES), 1) // cap

    def arrived(step):
        whole = [[], [], []]
        for h in range(tiles):
            sums = [jnp.zeros((8, LANES), jnp.float32)] * 3
            for o in range(h * per, (h + 1) * per):
                tile = pltpu.roll(recv[step, o], lax.rem(o - me + n * per, per) * cap, 1)
                for t, shift in enumerate((0, -1, 1)):
                    sums[t] = jnp.where(segment == (o + shift) % per, tile, sums[t])
            whole[0].append(sums[0])
            whole[1].append(pltpu.roll(sums[1], cap, 1))
            whole[2].append(pltpu.roll(sums[2], LANES - cap, 1))
        return [jnp.concatenate(w, axis=1) for w in whole]

    def fill(step, t, values, current):
        mine = row_of(place_rows[t], rows_of[t])
        parts = []
        for part in split2(values):
            wide = part.astype(jnp.float32)
            parts.append(
                jnp.concatenate(
                    [jnp.where(mine, wide[v : v + 1, :], 0.0) for v in range(nvar)], axis=0
                ).astype(jnp.bfloat16)
            )
        placed = sum(
            jnp.dot(part, spread[t], preferred_element_type=jnp.float32)
            for part in parts[::-1]
        )
        out = []
        for i, plane in enumerate(current):
            at = slice(i * columns, (i + 1) * columns)
            out.append(
                [
                    jnp.where(
                        fringe[t][at],
                        placed[v * rows_of[t] + i * columns : v * rows_of[t] + (i + 1) * columns],
                        plane[v],
                    )
                    for v in range(nvar)
                ]
            )
        return out

    def planes_of(ref):
        return [[ref[v, i] for v in range(nvar)] for i in range(planes)]

    def section(step, source, halo_pairs):
        both_sides(halo_pairs, "wait_recv")
        drain(step, recv_sem)
        values = arrived(step)
        own = fill(step, 0, values[0], planes_of(source))
        for i in range(planes):
            for v in range(nvar):
                filled[step, v, i] = own[i][v]
        left = fill(step, 1, values[1], [[halo[step, 0, v] for v in range(nvar)]])[0]
        right = fill(step, 2, values[2], [[halo[step, 1, v] for v in range(nvar)]])[0]
        left = [jnp.where(has_left, a, b) for a, b in zip(left, own[0])]
        right = [jnp.where(has_right, a, b) for a, b in zip(right, own[planes - 1])]
        cell = [primitive(u) for u in [left] + own + [right]]
        faces = [
            face(cell[i], cell[i + 1], tuple(normals[0, i, x] for x in range(4)))
            for i in range(planes + 1)
        ]
        stepped = []
        for i in range(planes):
            total = [b - a for a, b in zip(faces[i], faces[i + 1])]
            for g in (1, 2):
                more = difference_along(
                    cell[i + 1],
                    tuple(normals[g, i, x] for x in range(4)),
                    tuple(metrics[3 * g + x, i] for x in range(3)),
                    g - 1,
                )
                total = [a + b for a, b in zip(total, more)]
            factor = (-0.5 * TIME_STEP) * volume[i]
            update = jnp.logical_and(
                blank[i] == 1, jnp.logical_not(fringe[0][i * columns : (i + 1) * columns])
            )
            stepped.append((update, [factor * x for x in total]))
        return stepped

    for i, (update, change) in enumerate(section(0, state, halo_0)):
        for v in range(nvar):
            middle[v, i] = filled[0, v, i] + jnp.where(update, change[v], 0.0)
    halo_1 = [[copy] for copy in halo_copies(middle, 1)]
    both_sides(halo_1, "start")
    gather(middle, 1)
    exchange(1)
    for i, (update, change) in enumerate(section(1, middle, halo_1)):
        for v in range(nvar):
            end = filled[1, v, i]
            out_ref[v, i] = jnp.where(
                update, 0.5 * filled[0, v, i] + 0.5 * (end + change[v]), end
            )
    for step in range(2):
        drain(step, send_sem)
    for pairs in (halo_0, halo_1, once):
        both_sides(pairs, "wait_send")


def local(sizes, state, metrics, inv_volume, iblank, donor_cells, donor_fracs, receiver_cells):
    nvar, planes, columns, depth = state.shape
    slots = receiver_cells.shape[1]
    n = sizes[0] * sizes[1] * sizes[2]
    tiles = slots // LANES
    f32, bf16, i32 = jnp.float32, jnp.bfloat16, jnp.int32
    dma = pltpu.SemaphoreType.DMA
    return pl.pallas_call(
        functools.partial(kernel, sizes),
        out_shape=jax.ShapeDtypeStruct(state.shape, f32),
        in_specs=[pl.BlockSpec(memory_space=pltpu.HBM)] * 7,
        out_specs=pl.BlockSpec(memory_space=pltpu.VMEM),
        scratch_shapes=[
            pltpu.VMEM(state.shape, f32),
            pltpu.VMEM(metrics.shape, f32),
            pltpu.VMEM(inv_volume.shape, f32),
            pltpu.VMEM(iblank.shape, i32),
            pltpu.VMEM(donor_cells.shape, i32),
            pltpu.VMEM((3, 1, slots), f32),
            pltpu.VMEM(receiver_cells.shape, i32),
            pltpu.VMEM((depth, 2 * slots), bf16),
            pltpu.VMEM((3, slots, depth), bf16),
            pltpu.VMEM((2, tiles, 8, LANES), f32),
            pltpu.VMEM((2, n, 8, LANES), f32),
            pltpu.VMEM((2, 2, nvar, columns, depth), f32),
            pltpu.VMEM((2, 3, columns, depth), f32),
            pltpu.VMEM((2, 1, slots), i32),
            pltpu.VMEM((2,) + state.shape, f32),
            pltpu.VMEM(state.shape, f32),
            pltpu.VMEM((3, planes + 1, 4, columns, depth), f32),
            pltpu.VMEM((planes, columns, slots), f32),
            dma((7,)),
            dma((2,)),
            dma((2,)),
            dma((2, 2)),
            dma((2, 2)),
            dma((2, 2)),
            dma((2, 2)),
        ],
        compiler_params=pltpu.CompilerParams(
            collective_id=0, has_side_effects=True, vmem_limit_bytes=40 * 1024 * 1024
        ),
    )(
        *(
            pltpu.with_memory_space_constraint(x, pltpu.HBM)
            for x in (
                state, metrics, inv_volume, iblank, donor_cells,
                donor_fracs.reshape(3, 1, slots), receiver_cells,
            )
        )
    )


def solution(mesh):
    sizes = tuple(mesh.shape[axis] for axis in GROUP)
    return jax.shard_map(
        functools.partial(local, sizes),
        mesh=mesh,
        in_specs=(
            P(None, ("cases", "blocks", "split", "inner"), None, None),
            P(None, ("blocks", "split", "inner"), None, None),
            P(("blocks", "split", "inner"), None, None),
            P(("blocks", "split", "inner"), None, None),
            P(("blocks", "split", "inner"), None, None),
            P(("blocks", "split", "inner"), None, None),
            P(("blocks", "split", "inner"), None),
        ),
        out_specs=P(None, ("cases", "blocks", "split", "inner"), None, None),
        check_vma=False,
    )
```

```python
import functools

import jax
import jax.numpy as jnp
from jax import lax
from jax.experimental import pallas as pl
from jax.experimental.pallas import tpu as pltpu
from jax.sharding import PartitionSpec as P

HEAT_RATIO = 1.4
TIME_STEP = 0.08
GROUP = ("blocks", "split", "inner")
LANES = 128
MESH = pl.DeviceIdType.MESH


def split2(x):
    high = x.astype(jnp.bfloat16)
    rest = x - high.astype(jnp.float32)
    return high, rest.astype(jnp.bfloat16)


def primitive(u):
    density, m0, m1, m2, energy = u
    inverse = 1.0 / density
    pressure = (HEAT_RATIO - 1.0) * (energy - 0.5 * (m0 * m0 + m1 * m1 + m2 * m2) * inverse)
    sound = jnp.sqrt(HEAT_RATIO * pressure * inverse)
    return (density, m0, m1, m2, energy, inverse, pressure, sound)


def face(left, right, normal):
    n0, n1, n2, length = normal
    dl, al, bl, cl, el, il, pl_, sl = left
    dr, ar, br, cr, er, ir, pr, sr = right
    flow_l = al * n0 + bl * n1 + cl * n2
    flow_r = ar * n0 + br * n1 + cr * n2
    wl = flow_l * il
    wr = flow_r * ir
    radius = jnp.maximum(jnp.abs(wl) + sl * length, jnp.abs(wr) + sr * length)
    both = pl_ + pr
    return (
        flow_l + flow_r - radius * (dr - dl),
        al * wl + ar * wr + both * n0 - radius * (ar - al),
        bl * wl + br * wr + both * n1 - radius * (br - bl),
        cl * wl + cr * wr + both * n2 - radius * (cr - cl),
        (el + pl_) * wl + (er + pr) * wr - radius * (er - el),
    )


def twice_flux(cell, normal):
    n0, n1, n2 = (2.0 * n for n in normal)
    _, a, b, c, e, inverse, p, _ = cell
    flow = a * n0 + b * n1 + c * n2
    w = flow * inverse
    return (flow, a * w + p * n0, b * w + p * n1, c * w + p * n2, (e + p) * w)


def next_along(x, axis):
    size = x.shape[axis]
    index = lax.broadcasted_iota(jnp.int32, x.shape, axis)
    return jnp.where(index == size - 1, x, pltpu.roll(x, size - 1, axis))


def averaged(first, second):
    n = tuple(0.5 * (a + b) for a, b in zip(first, second))
    return n + (jnp.sqrt(n[0] * n[0] + n[1] * n[1] + n[2] * n[2]),)


def difference_along(cell, upper_normal, own_normal, axis):
    upper = face(cell, tuple(next_along(x, axis) for x in cell), upper_normal)
    span = 8 if axis == 0 else LANES
    cut = functools.partial(lax.slice_in_dim, start_index=0, limit_index=span, axis=axis)
    ghost = twice_flux(tuple(cut(x) for x in cell), tuple(cut(x) for x in own_normal))
    out = []
    for value, edge in zip(upper, ghost):
        lower = pltpu.roll(value, 1, axis)
        index = lax.broadcasted_iota(jnp.int32, edge.shape, axis)
        first = jnp.where(index == 0, edge, cut(lower))
        rest = lax.slice_in_dim(lower, span, lower.shape[axis], axis=axis)
        out.append(value - jnp.concatenate([first, rest], axis=axis))
    return out


def kernel(
    sizes,
    state_hbm, metrics_hbm, volume_hbm, blank_hbm, cells_hbm, fracs_hbm, targets_hbm,
    out_ref,
    state, metrics, volume, blank, cells, fracs, targets,
    hot, spread, send, recv, halo, halo_metrics, halo_targets, filled, middle, normals, marks,
    load_sem, send_sem, recv_sem, halo_send, halo_recv, once_send, once_recv,
):
    blocks, splits, inners = sizes
    n = blocks * splits * inners
    line = splits * inners
    nvar, planes, columns, depth = state.shape
    slots = targets.shape[1]
    cap = slots // n
    per = LANES // cap
    tiles = slots // LANES

    place = lax.axis_index("split") * inners + lax.axis_index("inner")
    me = lax.axis_index("blocks") * line + place
    has_left = place > 0
    has_right = place < line - 1

    def peer(r):
        return {"blocks": r // line, "split": (r // inners) % splits, "inner": r % inners}

    def beside(step):
        q = place + step
        return {"split": q // inners, "inner": q % inners}

    loads = [
        pltpu.make_async_copy(src, dst, load_sem.at[i])
        for i, (src, dst) in enumerate(
            (
                (cells_hbm, cells), (fracs_hbm, fracs), (state_hbm, state), (targets_hbm, targets),
                (metrics_hbm, metrics), (volume_hbm, volume), (blank_hbm, blank),
            )
        )
    ]
    bits = n.bit_length() - 1
    if n == 1 << bits:
        digits = [(me // (1 << b)) % 2 for b in range(bits)]
        others = [
            sum(((1 - digits[b]) if (mask >> b) % 2 else digits[b]) * (1 << b) for b in range(bits))
            for mask in range(n - 1, 0, -1)
        ]
    else:
        others = [lax.rem(me + d, n) for d in range(1, n)]
    barrier = pltpu.get_barrier_semaphore()
    for r in others:
        pl.semaphore_signal(barrier, inc=1, device_id=peer(r), device_id_type=MESH)
    for load in loads:
        load.start()

    def row_of(index, length):
        return lax.broadcasted_iota(jnp.int32, (length, slots), 0) == index

    def one_hot(index, length):
        return jnp.where(row_of(index, length), 1.0, 0.0)

    loads[0].wait()
    loads[1].wait()
    corner = cells[0, 0:1, :]
    k0 = corner % depth
    j0 = (corner // depth) % columns
    i0 = corner // (depth * columns)
    f0, f1, f2 = (fracs[g] for g in range(3))
    hot[:, 0:slots] = one_hot(k0, depth).astype(jnp.bfloat16)
    hot[:, slots : 2 * slots] = one_hot(k0 + 1, depth).astype(jnp.bfloat16)
    weight_j = one_hot(j0, columns) * (1.0 - f1) + one_hot(j0 + 1, columns) * f1
    weight_i = [
        jnp.where(i0 == i, 1.0 - f0, 0.0) + jnp.where(i0 + 1 == i, f0, 0.0)
        for i in range(planes)
    ]
    for i in range(planes):
        marks[i] = weight_j * weight_i[i]

    def gather(source, step):
        rows = nvar * planes * columns
        flat = source[...].reshape(rows, depth)
        parts = split2(flat)
        picked = sum(
            jnp.dot(part, hot[...], preferred_element_type=jnp.float32) for part in parts[::-1]
        )
        along = picked[:, 0:slots] * (1.0 - f2) + picked[:, slots : 2 * slots] * f2
        along = along.reshape(nvar, planes, columns, slots)
        for v in range(nvar):
            total = along[v, 0] * marks[0]
            for i in range(1, planes):
                total = total + along[v, i] * marks[i]
            row = jnp.sum(total, axis=0, keepdims=True)
            for h in range(tiles):
                send[step, h, v : v + 1, :] = row[:, h * LANES : (h + 1) * LANES]

    def exchange(step):
        copies = []
        for r in others:
            copies.append(
                pltpu.make_async_remote_copy(
                    src_ref=send.at[step, r // per],
                    dst_ref=recv.at[step, me],
                    send_sem=send_sem.at[step],
                    recv_sem=recv_sem.at[step],
                    device_id=peer(r),
                    device_id_type=MESH,
                )
            )
        for copy in copies:
            copy.start()
        recv[step, me] = send[step, me // per]

    def drain(step, sem):
        pltpu.make_async_copy(
            recv.at[step, pl.ds(0, n - 1)], recv.at[step, pl.ds(0, n - 1)], sem.at[step]
        ).wait()

    def halo_copies(source, step):
        return [
            pltpu.make_async_remote_copy(
                src_ref=source.at[:, 0 if side else planes - 1],
                dst_ref=halo.at[step, side],
                send_sem=halo_send.at[step, side],
                recv_sem=halo_recv.at[step, side],
                device_id=beside(-1 if side else 1),
                device_id_type=MESH,
            )
            for side in range(2)
        ]

    def once_copies():
        out = []
        for side in range(2):
            for item, (src, dst) in enumerate(
                (
                    (targets, halo_targets.at[side]),
                    (metrics.at[pl.ds(0, 3), 0 if side else planes - 1], halo_metrics.at[side]),
                )
            ):
                out.append(
                    pltpu.make_async_remote_copy(
                        src_ref=src,
                        dst_ref=dst,
                        send_sem=once_send.at[side, item],
                        recv_sem=once_recv.at[side, item],
                        device_id=beside(-1 if side else 1),
                        device_id_type=MESH,
                    )
                )
        return out[:2], out[2:]

    def both_sides(pairs, act):
        for side, sends in ((0, has_right), (1, has_left)):

            @pl.when(sends if act in ("start", "wait_send") else (has_left, has_right)[side])
            def _():
                for copy in pairs[side]:
                    getattr(copy, act)()

    loads[2].wait()
    gather(state, 0)
    for load in loads[3:5]:
        load.wait()
    pl.semaphore_wait(barrier, n - 1)
    exchange(0)
    once = once_copies()
    halo_0 = [[copy] for copy in halo_copies(state, 0)]
    both_sides(halo_0, "start")
    both_sides(once, "start")

    for i in range(planes):
        for g in (1, 2):
            own = tuple(metrics[3 * g + x, i] for x in range(3))
            mean = averaged(own, tuple(next_along(x, g - 1) for x in own))
            for x in range(4):
                normals[g, i, x] = mean[x]

    def spread_of(index, cell):
        spread[index] = one_hot(cell % depth, depth).T.astype(jnp.bfloat16)

    spread_of(0, targets[...])
    for load in loads[5:]:
        load.wait()
    both_sides(once, "wait_recv")
    for side in range(2):
        spread_of(1 + side, halo_targets[side])
    place_rows = [
        targets[...] // depth,
        halo_targets[0] // depth - (planes - 1) * columns,
        halo_targets[1] // depth,
    ]
    rows_of = [planes * columns, columns, columns]
    fringe = []
    for t in range(3):
        found = jnp.dot(
            one_hot(place_rows[t], rows_of[t]).astype(jnp.bfloat16), spread[t],
            preferred_element_type=jnp.float32,
        )
        fringe.append(found > 0.5)

    first = [metrics[x, 0] for x in range(3)]
    last = [metrics[x, planes - 1] for x in range(3)]
    line_normals = [
        tuple(jnp.where(has_left, halo_metrics[0, x], first[x]) for x in range(3))
    ]
    for i in range(planes):
        line_normals.append(tuple(metrics[x, i] for x in range(3)))
    line_normals.append(
        tuple(jnp.where(has_right, halo_metrics[1, x], last[x]) for x in range(3))
    )
    for i in range(planes + 1):
        mean = averaged(line_normals[i], line_normals[i + 1])
        for x in range(4):
            normals[0, i, x] = mean[x]

    segment = lax.broadcasted_iota(jnp.int32, (8, LANES), 1) // cap

    def arrived(step):
        whole = [[], [], []]
        for h in range(tiles):
            sums = [jnp.zeros((8, LANES), jnp.float32)] * 3
            for o in range(h * per, (h + 1) * per):
                tile = pltpu.roll(recv[step, o], lax.rem(o - me + n * per, per) * cap, 1)
                for t, shift in enumerate((0, -1, 1)):
                    sums[t] = jnp.where(segment == (o + shift) % per, tile, sums[t])
            whole[0].append(sums[0])
            whole[1].append(pltpu.roll(sums[1], cap, 1))
            whole[2].append(pltpu.roll(sums[2], LANES - cap, 1))
        return [jnp.concatenate(w, axis=1) for w in whole]

    def fill(step, t, values, current):
        mine = row_of(place_rows[t], rows_of[t])
        parts = []
        for part in split2(values):
            wide = part.astype(jnp.float32)
            parts.append(
                jnp.concatenate(
                    [jnp.where(mine, wide[v : v + 1, :], 0.0) for v in range(nvar)], axis=0
                ).astype(jnp.bfloat16)
            )
        placed = sum(
            jnp.dot(part, spread[t], preferred_element_type=jnp.float32)
            for part in parts[::-1]
        )
        out = []
        for i, plane in enumerate(current):
            at = slice(i * columns, (i + 1) * columns)
            out.append(
                [
                    jnp.where(
                        fringe[t][at],
                        placed[v * rows_of[t] + i * columns : v * rows_of[t] + (i + 1) * columns],
                        plane[v],
                    )
                    for v in range(nvar)
                ]
            )
        return out

    def planes_of(ref):
        return [[ref[v, i] for v in range(nvar)] for i in range(planes)]

    def section(step, source, halo_pairs):
        both_sides(halo_pairs, "wait_recv")
        drain(step, recv_sem)
        values = arrived(step)
        own = fill(step, 0, values[0], planes_of(source))
        for i in range(planes):
            for v in range(nvar):
                filled[step, v, i] = own[i][v]
        left = fill(step, 1, values[1], [[halo[step, 0, v] for v in range(nvar)]])[0]
        right = fill(step, 2, values[2], [[halo[step, 1, v] for v in range(nvar)]])[0]
        left = [jnp.where(has_left, a, b) for a, b in zip(left, own[0])]
        right = [jnp.where(has_right, a, b) for a, b in zip(right, own[planes - 1])]
        cell = [primitive(u) for u in [left] + own + [right]]
        faces = [
            face(cell[i], cell[i + 1], tuple(normals[0, i, x] for x in range(4)))
            for i in range(planes + 1)
        ]
        stepped = []
        for i in range(planes):
            total = [b - a for a, b in zip(faces[i], faces[i + 1])]
            for g in (1, 2):
                more = difference_along(
                    cell[i + 1],
                    tuple(normals[g, i, x] for x in range(4)),
                    tuple(metrics[3 * g + x, i] for x in range(3)),
                    g - 1,
                )
                total = [a + b for a, b in zip(total, more)]
            factor = (-0.5 * TIME_STEP) * volume[i]
            update = jnp.logical_and(
                blank[i] == 1, jnp.logical_not(fringe[0][i * columns : (i + 1) * columns])
            )
            stepped.append((update, [factor * x for x in total]))
        return stepped

    for i, (update, change) in enumerate(section(0, state, halo_0)):
        for v in range(nvar):
            middle[v, i] = filled[0, v, i] + jnp.where(update, change[v], 0.0)
    halo_1 = [[copy] for copy in halo_copies(middle, 1)]
    gather(middle, 1)
    exchange(1)
    both_sides(halo_1, "start")
    for i, (update, change) in enumerate(section(1, middle, halo_1)):
        for v in range(nvar):
            end = filled[1, v, i]
            out_ref[v, i] = jnp.where(
                update, 0.5 * filled[0, v, i] + 0.5 * (end + change[v]), end
            )
    for step in range(2):
        drain(step, send_sem)
    for pairs in (halo_0, halo_1, once):
        both_sides(pairs, "wait_send")


def local(sizes, state, metrics, inv_volume, iblank, donor_cells, donor_fracs, receiver_cells):
    nvar, planes, columns, depth = state.shape
    slots = receiver_cells.shape[1]
    n = sizes[0] * sizes[1] * sizes[2]
    tiles = slots // LANES
    f32, bf16, i32 = jnp.float32, jnp.bfloat16, jnp.int32
    dma = pltpu.SemaphoreType.DMA
    return pl.pallas_call(
        functools.partial(kernel, sizes),
        out_shape=jax.ShapeDtypeStruct(state.shape, f32),
        in_specs=[pl.BlockSpec(memory_space=pltpu.HBM)] * 7,
        out_specs=pl.BlockSpec(memory_space=pltpu.VMEM),
        scratch_shapes=[
            pltpu.VMEM(state.shape, f32),
            pltpu.VMEM(metrics.shape, f32),
            pltpu.VMEM(inv_volume.shape, f32),
            pltpu.VMEM(iblank.shape, i32),
            pltpu.VMEM(donor_cells.shape, i32),
            pltpu.VMEM((3, 1, slots), f32),
            pltpu.VMEM(receiver_cells.shape, i32),
            pltpu.VMEM((depth, 2 * slots), bf16),
            pltpu.VMEM((3, slots, depth), bf16),
            pltpu.VMEM((2, tiles, 8, LANES), f32),
            pltpu.VMEM((2, n, 8, LANES), f32),
            pltpu.VMEM((2, 2, nvar, columns, depth), f32),
            pltpu.VMEM((2, 3, columns, depth), f32),
            pltpu.VMEM((2, 1, slots), i32),
            pltpu.VMEM((2,) + state.shape, f32),
            pltpu.VMEM(state.shape, f32),
            pltpu.VMEM((3, planes + 1, 4, columns, depth), f32),
            pltpu.VMEM((planes, columns, slots), f32),
            dma((7,)),
            dma((2,)),
            dma((2,)),
            dma((2, 2)),
            dma((2, 2)),
            dma((2, 2)),
            dma((2, 2)),
        ],
        compiler_params=pltpu.CompilerParams(
            collective_id=0, has_side_effects=True, vmem_limit_bytes=40 * 1024 * 1024
        ),
    )(
        *(
            pltpu.with_memory_space_constraint(x, pltpu.HBM)
            for x in (
                state, metrics, inv_volume, iblank, donor_cells,
                donor_fracs.reshape(3, 1, slots), receiver_cells,
            )
        )
    )


def solution(mesh):
    sizes = tuple(mesh.shape[axis] for axis in GROUP)
    return jax.shard_map(
        functools.partial(local, sizes),
        mesh=mesh,
        in_specs=(
            P(None, ("cases", "blocks", "split", "inner"), None, None),
            P(None, ("blocks", "split", "inner"), None, None),
            P(("blocks", "split", "inner"), None, None),
            P(("blocks", "split", "inner"), None, None),
            P(("blocks", "split", "inner"), None, None),
            P(("blocks", "split", "inner"), None, None),
            P(("blocks", "split", "inner"), None),
        ),
        out_specs=P(None, ("cases", "blocks", "split", "inner"), None, None),
        check_vma=False,
    )
```

```python
import functools

import jax
import jax.numpy as jnp
from jax import lax
from jax.experimental import pallas as pl
from jax.experimental.pallas import tpu as pltpu
from jax.sharding import PartitionSpec as P

HEAT_RATIO = 1.4
TIME_STEP = 0.08
GROUP = ("blocks", "split", "inner")
LANES = 128
MESH = pl.DeviceIdType.MESH


def split2(x):
    high = x.astype(jnp.bfloat16)
    rest = x - high.astype(jnp.float32)
    return high, rest.astype(jnp.bfloat16)


def primitive(u):
    density, m0, m1, m2, energy = u
    inverse = 1.0 / density
    pressure = (HEAT_RATIO - 1.0) * (energy - 0.5 * (m0 * m0 + m1 * m1 + m2 * m2) * inverse)
    sound = jnp.sqrt(HEAT_RATIO * pressure * inverse)
    return (density, m0, m1, m2, energy, inverse, pressure, sound)


def face(left, right, normal):
    n0, n1, n2, length = normal
    dl, al, bl, cl, el, il, pl_, sl = left
    dr, ar, br, cr, er, ir, pr, sr = right
    flow_l = al * n0 + bl * n1 + cl * n2
    flow_r = ar * n0 + br * n1 + cr * n2
    wl = flow_l * il
    wr = flow_r * ir
    radius = jnp.maximum(jnp.abs(wl) + sl * length, jnp.abs(wr) + sr * length)
    both = pl_ + pr
    return (
        flow_l + flow_r - radius * (dr - dl),
        al * wl + ar * wr + both * n0 - radius * (ar - al),
        bl * wl + br * wr + both * n1 - radius * (br - bl),
        cl * wl + cr * wr + both * n2 - radius * (cr - cl),
        (el + pl_) * wl + (er + pr) * wr - radius * (er - el),
    )


def twice_flux(cell, normal):
    n0, n1, n2 = (2.0 * n for n in normal)
    _, a, b, c, e, inverse, p, _ = cell
    flow = a * n0 + b * n1 + c * n2
    w = flow * inverse
    return (flow, a * w + p * n0, b * w + p * n1, c * w + p * n2, (e + p) * w)


def next_along(x, axis):
    size = x.shape[axis]
    index = lax.broadcasted_iota(jnp.int32, x.shape, axis)
    return jnp.where(index == size - 1, x, pltpu.roll(x, size - 1, axis))


def averaged(first, second):
    n = tuple(0.5 * (a + b) for a, b in zip(first, second))
    return n + (jnp.sqrt(n[0] * n[0] + n[1] * n[1] + n[2] * n[2]),)


def difference_along(cell, upper_normal, own_normal, axis):
    upper = face(cell, tuple(next_along(x, axis) for x in cell), upper_normal)
    span = 8 if axis == 0 else LANES
    cut = functools.partial(lax.slice_in_dim, start_index=0, limit_index=span, axis=axis)
    ghost = twice_flux(tuple(cut(x) for x in cell), tuple(cut(x) for x in own_normal))
    out = []
    for value, edge in zip(upper, ghost):
        lower = pltpu.roll(value, 1, axis)
        index = lax.broadcasted_iota(jnp.int32, edge.shape, axis)
        first = jnp.where(index == 0, edge, cut(lower))
        rest = lax.slice_in_dim(lower, span, lower.shape[axis], axis=axis)
        out.append(value - jnp.concatenate([first, rest], axis=axis))
    return out


def kernel(
    sizes,
    state_hbm, metrics_hbm, volume_hbm, blank_hbm, cells_hbm, fracs_hbm, targets_hbm,
    out_ref,
    state, metrics, volume, blank, cells, fracs, targets,
    hot, spread, send, recv, halo, halo_metrics, halo_targets, filled, middle, normals, marks,
    load_sem, send_sem, recv_sem, halo_send, halo_recv, once_send, once_recv,
):
    blocks, splits, inners = sizes
    n = blocks * splits * inners
    line = splits * inners
    nvar, planes, columns, depth = state.shape
    slots = targets.shape[1]
    cap = slots // n
    per = LANES // cap
    tiles = slots // LANES

    place = lax.axis_index("split") * inners + lax.axis_index("inner")
    me = lax.axis_index("blocks") * line + place
    has_left = place > 0
    has_right = place < line - 1

    def peer(r):
        return {"blocks": r // line, "split": (r // inners) % splits, "inner": r % inners}

    def beside(step):
        q = place + step
        return {"split": q // inners, "inner": q % inners}

    loads = [
        pltpu.make_async_copy(src, dst, load_sem.at[i])
        for i, (src, dst) in enumerate(
            (
                (cells_hbm, cells), (fracs_hbm, fracs), (state_hbm, state), (targets_hbm, targets),
                (metrics_hbm, metrics), (volume_hbm, volume), (blank_hbm, blank),
            )
        )
    ]
    bits = n.bit_length() - 1
    if n == 1 << bits:
        digits = [(me // (1 << b)) % 2 for b in range(bits)]
        others = [
            sum(((1 - digits[b]) if (mask >> b) % 2 else digits[b]) * (1 << b) for b in range(bits))
            for mask in range(n - 1, 0, -1)
        ]
    else:
        others = [lax.rem(me + d, n) for d in range(1, n)]
    barrier = pltpu.get_barrier_semaphore()
    for r in others:
        pl.semaphore_signal(barrier, inc=1, device_id=peer(r), device_id_type=MESH)
    for load in loads:
        load.start()

    def row_of(index, length):
        return lax.broadcasted_iota(jnp.int32, (length, slots), 0) == index

    def one_hot(index, length):
        return jnp.where(row_of(index, length), 1.0, 0.0)

    loads[0].wait()
    loads[1].wait()
    corner = cells[0, 0:1, :]
    k0 = corner % depth
    j0 = (corner // depth) % columns
    i0 = corner // (depth * columns)
    f0, f1, f2 = (fracs[g] for g in range(3))
    hot[:, 0:slots] = one_hot(k0, depth).astype(jnp.bfloat16)
    hot[:, slots : 2 * slots] = one_hot(k0 + 1, depth).astype(jnp.bfloat16)
    weight_j = one_hot(j0, columns) * (1.0 - f1) + one_hot(j0 + 1, columns) * f1
    weight_i = [
        jnp.where(i0 == i, 1.0 - f0, 0.0) + jnp.where(i0 + 1 == i, f0, 0.0)
        for i in range(planes)
    ]
    for i in range(planes):
        marks[i] = weight_j * weight_i[i]

    def gather(source, step):
        rows = nvar * planes * columns
        flat = source[...].reshape(rows, depth)
        parts = split2(flat)
        picked = sum(
            jnp.dot(part, hot[...], preferred_element_type=jnp.float32) for part in parts[::-1]
        )
        along = picked[:, 0:slots] * (1.0 - f2) + picked[:, slots : 2 * slots] * f2
        along = along.reshape(nvar, planes, columns, slots)
        for v in range(nvar):
            total = along[v, 0] * marks[0]
            for i in range(1, planes):
                total = total + along[v, i] * marks[i]
            row = jnp.sum(total, axis=0, keepdims=True)
            for h in range(tiles):
                send[step, h, v : v + 1, :] = row[:, h * LANES : (h + 1) * LANES]

    def exchange(step):
        copies = []
        for r in others:
            copies.append(
                pltpu.make_async_remote_copy(
                    src_ref=send.at[step, r // per],
                    dst_ref=recv.at[step, me],
                    send_sem=send_sem.at[step],
                    recv_sem=recv_sem.at[step],
                    device_id=peer(r),
                    device_id_type=MESH,
                )
            )
        for copy in copies:
            copy.start()
        recv[step, me] = send[step, me // per]

    def drain(step, sem):
        pltpu.make_async_copy(
            recv.at[step, pl.ds(0, n - 1)], recv.at[step, pl.ds(0, n - 1)], sem.at[step]
        ).wait()

    def halo_copies(source, step):
        return [
            pltpu.make_async_remote_copy(
                src_ref=source.at[:, 0 if side else planes - 1],
                dst_ref=halo.at[step, side],
                send_sem=halo_send.at[step, side],
                recv_sem=halo_recv.at[step, side],
                device_id=beside(-1 if side else 1),
                device_id_type=MESH,
            )
            for side in range(2)
        ]

    def once_copies():
        out = []
        for side in range(2):
            for item, (src, dst) in enumerate(
                (
                    (targets, halo_targets.at[side]),
                    (metrics.at[pl.ds(0, 3), 0 if side else planes - 1], halo_metrics.at[side]),
                )
            ):
                out.append(
                    pltpu.make_async_remote_copy(
                        src_ref=src,
                        dst_ref=dst,
                        send_sem=once_send.at[side, item],
                        recv_sem=once_recv.at[side, item],
                        device_id=beside(-1 if side else 1),
                        device_id_type=MESH,
                    )
                )
        return out[:2], out[2:]

    def both_sides(pairs, act):
        for side, sends in ((0, has_right), (1, has_left)):

            @pl.when(sends if act in ("start", "wait_send") else (has_left, has_right)[side])
            def _():
                for copy in pairs[side]:
                    getattr(copy, act)()

    loads[2].wait()
    gather(state, 0)
    for load in loads[3:5]:
        load.wait()
    pl.semaphore_wait(barrier, n - 1)
    exchange(0)
    once = once_copies()
    halo_0 = [[copy] for copy in halo_copies(state, 0)]
    both_sides(once, "start")
    both_sides(halo_0, "start")

    for i in range(planes):
        for g in (1, 2):
            own = tuple(metrics[3 * g + x, i] for x in range(3))
            mean = averaged(own, tuple(next_along(x, g - 1) for x in own))
            for x in range(4):
                normals[g, i, x] = mean[x]

    def spread_of(index, cell):
        spread[index] = one_hot(cell % depth, depth).T.astype(jnp.bfloat16)

    spread_of(0, targets[...])
    for load in loads[5:]:
        load.wait()
    both_sides(once, "wait_recv")
    for side in range(2):
        spread_of(1 + side, halo_targets[side])
    place_rows = [
        targets[...] // depth,
        halo_targets[0] // depth - (planes - 1) * columns,
        halo_targets[1] // depth,
    ]
    rows_of = [planes * columns, columns, columns]
    fringe = []
    for t in range(3):
        found = jnp.dot(
            one_hot(place_rows[t], rows_of[t]).astype(jnp.bfloat16), spread[t],
            preferred_element_type=jnp.float32,
        )
        fringe.append(found > 0.5)

    first = [metrics[x, 0] for x in range(3)]
    last = [metrics[x, planes - 1] for x in range(3)]
    line_normals = [
        tuple(jnp.where(has_left, halo_metrics[0, x], first[x]) for x in range(3))
    ]
    for i in range(planes):
        line_normals.append(tuple(metrics[x, i] for x in range(3)))
    line_normals.append(
        tuple(jnp.where(has_right, halo_metrics[1, x], last[x]) for x in range(3))
    )
    for i in range(planes + 1):
        mean = averaged(line_normals[i], line_normals[i + 1])
        for x in range(4):
            normals[0, i, x] = mean[x]

    segment = lax.broadcasted_iota(jnp.int32, (8, LANES), 1) // cap

    def arrived(step):
        whole = [[], [], []]
        for h in range(tiles):
            sums = [jnp.zeros((8, LANES), jnp.float32)] * 3
            for o in range(h * per, (h + 1) * per):
                tile = pltpu.roll(recv[step, o], lax.rem(o - me + n * per, per) * cap, 1)
                for t, shift in enumerate((0, -1, 1)):
                    sums[t] = jnp.where(segment == (o + shift) % per, tile, sums[t])
            whole[0].append(sums[0])
            whole[1].append(pltpu.roll(sums[1], cap, 1))
            whole[2].append(pltpu.roll(sums[2], LANES - cap, 1))
        return [jnp.concatenate(w, axis=1) for w in whole]

    def fill(step, t, values, current):
        mine = row_of(place_rows[t], rows_of[t])
        parts = []
        for part in split2(values):
            wide = part.astype(jnp.float32)
            parts.append(
                jnp.concatenate(
                    [jnp.where(mine, wide[v : v + 1, :], 0.0) for v in range(nvar)], axis=0
                ).astype(jnp.bfloat16)
            )
        placed = sum(
            jnp.dot(part, spread[t], preferred_element_type=jnp.float32)
            for part in parts[::-1]
        )
        out = []
        for i, plane in enumerate(current):
            at = slice(i * columns, (i + 1) * columns)
            out.append(
                [
                    jnp.where(
                        fringe[t][at],
                        placed[v * rows_of[t] + i * columns : v * rows_of[t] + (i + 1) * columns],
                        plane[v],
                    )
                    for v in range(nvar)
                ]
            )
        return out

    def planes_of(ref):
        return [[ref[v, i] for v in range(nvar)] for i in range(planes)]

    def section(step, source, halo_pairs):
        both_sides(halo_pairs, "wait_recv")
        drain(step, recv_sem)
        values = arrived(step)
        own = fill(step, 0, values[0], planes_of(source))
        for i in range(planes):
            for v in range(nvar):
                filled[step, v, i] = own[i][v]
        left = fill(step, 1, values[1], [[halo[step, 0, v] for v in range(nvar)]])[0]
        right = fill(step, 2, values[2], [[halo[step, 1, v] for v in range(nvar)]])[0]
        left = [jnp.where(has_left, a, b) for a, b in zip(left, own[0])]
        right = [jnp.where(has_right, a, b) for a, b in zip(right, own[planes - 1])]
        cell = [primitive(u) for u in [left] + own + [right]]
        faces = [
            face(cell[i], cell[i + 1], tuple(normals[0, i, x] for x in range(4)))
            for i in range(planes + 1)
        ]
        stepped = []
        for i in range(planes):
            total = [b - a for a, b in zip(faces[i], faces[i + 1])]
            for g in (1, 2):
                more = difference_along(
                    cell[i + 1],
                    tuple(normals[g, i, x] for x in range(4)),
                    tuple(metrics[3 * g + x, i] for x in range(3)),
                    g - 1,
                )
                total = [a + b for a, b in zip(total, more)]
            factor = (-0.5 * TIME_STEP) * volume[i]
            update = jnp.logical_and(
                blank[i] == 1, jnp.logical_not(fringe[0][i * columns : (i + 1) * columns])
            )
            stepped.append((update, [factor * x for x in total]))
        return stepped

    for i, (update, change) in enumerate(section(0, state, halo_0)):
        for v in range(nvar):
            middle[v, i] = filled[0, v, i] + jnp.where(update, change[v], 0.0)
    halo_1 = [[copy] for copy in halo_copies(middle, 1)]
    gather(middle, 1)
    exchange(1)
    both_sides(halo_1, "start")
    for i, (update, change) in enumerate(section(1, middle, halo_1)):
        for v in range(nvar):
            end = filled[1, v, i]
            out_ref[v, i] = jnp.where(
                update, 0.5 * filled[0, v, i] + 0.5 * (end + change[v]), end
            )
    for step in range(2):
        drain(step, send_sem)
    for pairs in (halo_0, halo_1, once):
        both_sides(pairs, "wait_send")


def local(sizes, state, metrics, inv_volume, iblank, donor_cells, donor_fracs, receiver_cells):
    nvar, planes, columns, depth = state.shape
    slots = receiver_cells.shape[1]
    n = sizes[0] * sizes[1] * sizes[2]
    tiles = slots // LANES
    f32, bf16, i32 = jnp.float32, jnp.bfloat16, jnp.int32
    dma = pltpu.SemaphoreType.DMA
    return pl.pallas_call(
        functools.partial(kernel, sizes),
        out_shape=jax.ShapeDtypeStruct(state.shape, f32),
        in_specs=[pl.BlockSpec(memory_space=pltpu.HBM)] * 7,
        out_specs=pl.BlockSpec(memory_space=pltpu.VMEM),
        scratch_shapes=[
            pltpu.VMEM(state.shape, f32),
            pltpu.VMEM(metrics.shape, f32),
            pltpu.VMEM(inv_volume.shape, f32),
            pltpu.VMEM(iblank.shape, i32),
            pltpu.VMEM(donor_cells.shape, i32),
            pltpu.VMEM((3, 1, slots), f32),
            pltpu.VMEM(receiver_cells.shape, i32),
            pltpu.VMEM((depth, 2 * slots), bf16),
            pltpu.VMEM((3, slots, depth), bf16),
            pltpu.VMEM((2, tiles, 8, LANES), f32),
            pltpu.VMEM((2, n, 8, LANES), f32),
            pltpu.VMEM((2, 2, nvar, columns, depth), f32),
            pltpu.VMEM((2, 3, columns, depth), f32),
            pltpu.VMEM((2, 1, slots), i32),
            pltpu.VMEM((2,) + state.shape, f32),
            pltpu.VMEM(state.shape, f32),
            pltpu.VMEM((3, planes + 1, 4, columns, depth), f32),
            pltpu.VMEM((planes, columns, slots), f32),
            dma((7,)),
            dma((2,)),
            dma((2,)),
            dma((2, 2)),
            dma((2, 2)),
            dma((2, 2)),
            dma((2, 2)),
        ],
        compiler_params=pltpu.CompilerParams(
            collective_id=0, has_side_effects=True, vmem_limit_bytes=40 * 1024 * 1024
        ),
    )(
        *(
            pltpu.with_memory_space_constraint(x, pltpu.HBM)
            for x in (
                state, metrics, inv_volume, iblank, donor_cells,
                donor_fracs.reshape(3, 1, slots), receiver_cells,
            )
        )
    )


def solution(mesh):
    sizes = tuple(mesh.shape[axis] for axis in GROUP)
    return jax.shard_map(
        functools.partial(local, sizes),
        mesh=mesh,
        in_specs=(
            P(None, ("cases", "blocks", "split", "inner"), None, None),
            P(None, ("blocks", "split", "inner"), None, None),
            P(("blocks", "split", "inner"), None, None),
            P(("blocks", "split", "inner"), None, None),
            P(("blocks", "split", "inner"), None, None),
            P(("blocks", "split", "inner"), None, None),
            P(("blocks", "split", "inner"), None),
        ),
        out_specs=P(None, ("cases", "blocks", "split", "inner"), None, None),
        check_vma=False,
    )
```
